512 devices in a mesh: own: 32 (over y, x), dp: 16 (over z, core).
Axes of the slice: x: 4, y: 8, z: 8, core: 2. Of those that a mesh axis runs over, the one named last changes fastest.
Arguments:
- acts: bfloat16 [4096, 2048], P('own', 'dp'), may hold values from -6 to 6
- grads_out: bfloat16 [4096, 15360], P('own', 'dp'), may hold values from -0.09375 to 0.09375
- stats: float32 [32, 16, 1, 512, 512], P('own', 'dp'), as said below
- owner: int32 [120, 1], replicated, may hold values from 0 to 31; in each aligned block of 30 rows (0 to 29, 30 to 59, ...) at most 2 rows name the same one
- col_index: int32 [4, 30], replicated, may hold values from 0 to 29, each once within a row
Outputs:
- update: bfloat16 [32, 16, 2, 128, 512], P('own', 'dp')
The draws below stay inside these ranges and needn't reach their ends.
Inputs may be any that keep to these rules, and one draw needn't show every extreme that they name: Within one block-row (aligned runs of 30 entries) no owner holds more than 2 blocks, and in some block-row an owner holds exactly 2. `col_index`: each row is a permutation. `stats`: each matrix is symmetric, and each diagonal entry exceeds the sum of magnitudes of the other entries of its row.
All inputs are finite; a program needn't handle non-finite values.
Results may differ from the reference program's by a relative error of at most 0.028.
Values may be sent and summed in bfloat16 or wider, within the bound.
A program may use at most 64 MiB of HBM per device.

```python
import math
import jax
import jax.numpy as jnp
import numpy as np
from jax import lax

BS = 512
QW = 15360
TOK_DEV = 128
XB = 4
XW = 2048
YB = 30
CAPR = 2
NB = 120
TOKENS = 4096
N_OWN = 32
N_DP = 16


def draw_stats(key, part):
    key = jax.random.fold_in(key, 11)
    diag_key, off_key = jax.random.split(key)
    shape = (N_OWN, N_DP, CAPR // 2, BS, BS)
    diagonal = jnp.exp(jax.random.uniform(diag_key, shape[:-1], jnp.float32, jnp.log(10.0), jnp.log(40.0)))
    bound = 9.0 / BS
    off = jax.random.uniform(off_key, shape, jnp.float32, -bound, bound)
    off = 0.5 * (off + jnp.swapaxes(off, -1, -2))
    identity = jnp.eye(BS, dtype=jnp.float32)
    return off * (1.0 - identity) + identity * diagonal[..., None]


def level_of(stream_key, dims, pieces, least, largest):
    factor_of = 1.0
    for dim, parts in pieces:
        draws = jax.random.uniform(jax.random.fold_in(jax.random.fold_in(stream_key, 6), dim), (parts,), jnp.float32, least / len(pieces), largest / len(pieces))
        factor_of = factor_of * jnp.repeat(jnp.exp(draws), dims[dim] // parts).reshape((-1,) + (1,) * (len(dims) - 1 - dim))
    return factor_of


def assign_block(stream_key, own, number, rows, count, top, most, skew):
    order = jax.random.permutation(stream_key, count)
    packed, common = shares(count, rows * top, most, skew, True), shares(count, rows * top, most, skew, False)
    places = jnp.arange(count)

    def named(sizes, turn):
        used = int((sizes > 0).sum())
        fixed = max(1, used // 4)
        shifted = fixed + (places - fixed + turn * (used - fixed)) % max(1, count - fixed)
        return jnp.zeros((count,), jnp.int32).at[order[jnp.where(places < fixed, places, shifted)]].set(jnp.asarray(sizes, jnp.int32))

    sizes = jnp.where(number % 4 == 0, named(packed, number // 4), named(common, number - number // 4 - 1))
    mixed = jax.random.permutation(jax.random.fold_in(own, 3), count)
    source_of, receiver = mixed[0:count // 2 * 2:2], mixed[1:count // 2 * 2:2]
    slack = jnp.minimum(sizes[source_of] - 1, most - sizes[receiver]) // 2
    slack = jnp.where((source_of == order[0]) | (receiver == order[0]) | (sizes[receiver] == 0), 0, jnp.maximum(slack, 0))
    shifted = jax.random.randint(jax.random.fold_in(own, 4), (count // 2,), 0, 1 << 20) % (slack + 1)
    sizes = sizes.at[source_of].add(-shifted).at[receiver].add(shifted)
    members = jnp.searchsorted(jnp.cumsum(sizes), jnp.arange(rows * top), side="right").astype(jnp.int32)
    table = members.reshape(top, rows).T
    table = table[jax.random.permutation(jax.random.fold_in(own, 1), rows)]
    turn = jax.random.randint(jax.random.fold_in(own, 2), (rows, 1), 0, top)
    return jnp.take_along_axis(table, (jnp.arange(top)[None, :] + turn) % top, axis=1)


def shares(amount, total, most, slope, full):
    portions = [(1 << 20) // math.isqrt(rank ** slope) + 1 for rank in range(1, amount + 1)]
    largest = most if full else min(most, max(-(-total // amount), total * portions[0] // sum(portions)))
    least = 1 if total - largest >= amount - 1 else 0
    holding, rest = [largest] + [least] * (amount - 1), total - largest - least * (amount - 1)
    while rest > 0:
        free = [i for i in range(1, amount) if holding[i] < largest] or [i for i in range(1, amount) if holding[i] < most]
        whole, remaining = sum([portions[i] for i in free]), rest
        for i in free:
            addition = min(most - holding[i], max(1, remaining * portions[i] // whole), rest)
            holding[i] = holding[i] + addition
            rest = rest - addition
    return np.array(holding)


def centred(stream_key, dims, width, most, pieces=(), held_as=jnp.bfloat16):
    result = jax.random.normal(stream_key, dims, jnp.float32) * width
    if len(pieces) > 0:
        result = level_of(stream_key, dims, pieces, -0.22, 0.18) * result
    return jnp.clip(result, min=-most, max=most).astype(held_as)


def setup_inputs(seed: int = 0) -> dict:
    arg_keys = jax.random.split(jax.random.key(seed), 6)
    acts = centred(arg_keys[0], (TOKENS, XW), 1.0, 6.0, ((0, 32), (1, 16)))
    grads_out = centred(arg_keys[1], (TOKENS, QW), TOKENS ** -0.5, 0.09375, ((0, 32), (1, 16)))
    stats = draw_stats(jax.random.fold_in(arg_keys[5], 71), 0)
    owner_keys = jax.random.split(jax.random.fold_in(arg_keys[3], 1), NB // YB)
    owner_turns = jax.random.permutation(jax.random.fold_in(arg_keys[3], 3), NB // YB)
    owner = jax.vmap(lambda own, number: assign_block(jax.random.fold_in(arg_keys[3], 2), own, number, YB, N_OWN, 1, CAPR, 2))(owner_keys, owner_turns).reshape((NB, 1))
    col_index = jax.vmap(lambda own: jax.random.permutation(own, YB))(jax.random.split(arg_keys[4], XB)).reshape((XB, YB)).astype(jnp.int32)
    return {"acts": acts, "grads_out": grads_out, "stats": stats, "owner": owner, "col_index": col_index}


STAT_DECAY = 0.9
EPSILON = 1e-06

def exact_product(left, right):
    return jnp.dot(left, right, precision=lax.Precision.HIGHEST)

def inverse_root(matrix):
    size = matrix.shape[0]
    identity = jnp.eye(size, dtype=matrix.dtype)
    scale = jnp.trace(matrix) / size + EPSILON
    start = matrix / scale
    first = (5.0 * identity - start) / 4.0
    square = exact_product(first, first)
    fourth = exact_product(square, square)
    moved = exact_product(fourth, start)
    second = (5.0 * identity - moved) / 4.0
    return exact_product(first, second)

def one_block(items):
    grad_block, left_old, right_old = items
    left_new = STAT_DECAY * left_old + (1.0 - STAT_DECAY) * jnp.dot(grad_block, grad_block.T, preferred_element_type=jnp.float32)
    right_new = STAT_DECAY * right_old + (1.0 - STAT_DECAY) * jnp.dot(grad_block.T, grad_block, preferred_element_type=jnp.float32)
    left_root = inverse_root(left_new).astype(jnp.bfloat16)
    right_root = inverse_root(right_new).astype(jnp.bfloat16)
    carried = jnp.dot(left_root, grad_block, preferred_element_type=jnp.float32).astype(jnp.bfloat16)
    precond = jnp.dot(carried, right_root, preferred_element_type=jnp.float32)
    wide = grad_block.astype(jnp.float32)
    grad_scale = jnp.sqrt(jnp.mean(wide * wide) + EPSILON)
    prec_scale = jnp.sqrt(jnp.mean(precond * precond) + EPSILON)
    return (precond * (grad_scale / prec_scale)).astype(jnp.bfloat16)

def reference(acts, grads_out, stats, owner, col_index):
    acts_split = acts.reshape(N_OWN, TOK_DEV, XW)
    grads_split = grads_out.reshape(N_OWN, TOK_DEV, QW)

    def accumulate(total, pair):
        part = jnp.dot(pair[0].T, pair[1], preferred_element_type=jnp.float32).astype(jnp.bfloat16)
        part = lax.optimization_barrier(part)
        return (total + part.astype(jnp.float32), None)
    total, _ = lax.scan(accumulate, jnp.zeros((XW, QW), jnp.float32), (acts_split, grads_split))
    gradient = total.astype(jnp.bfloat16)
    owners = owner[:, 0].reshape(XB, YB)
    positions = jnp.arange(YB, dtype=jnp.int32)
    same_owner = owners[:, :, None] == owners[:, None, :]
    earlier = positions[None, :] < positions[:, None]
    slots = lax.optimization_barrier(jnp.sum((same_owner & earlier[None]).astype(jnp.int32), axis=2))
    owner_hit = (owners[:, :, None] == jnp.arange(N_OWN, dtype=jnp.int32)[None, None, :]).astype(jnp.float32)
    slot_hit = (slots[:, :, None] == jnp.arange(CAPR, dtype=jnp.int32)[None, None, :]).astype(jnp.float32)
    column_hit = (col_index[:, :, None] == positions[None, None, :]).astype(jnp.float32)
    select = jnp.einsum('iko,iks,ikp->iosp', owner_hit, slot_hit, column_hit)
    grid = gradient.astype(jnp.float32).reshape(XB, BS, YB, BS)
    blocks = jnp.einsum('iosp,iapb->oisab', select, grid).astype(jnp.bfloat16)
    blocks = blocks.reshape(N_OWN * XB * CAPR, BS, BS)
    arranged = stats.reshape(N_OWN, XB, 4, CAPR // 2, BS, BS).transpose(0, 1, 3, 2, 4, 5)
    arranged = arranged.reshape(N_OWN, XB, CAPR, 2, BS, BS)
    left_stats = arranged[:, :, :, 0].reshape(N_OWN * XB * CAPR, BS, BS)
    right_stats = arranged[:, :, :, 1].reshape(N_OWN * XB * CAPR, BS, BS)
    updates = lax.map(one_block, (blocks, left_stats, right_stats))
    updates = updates.reshape(N_OWN, XB, CAPR, 4, BS // 4, BS).transpose(0, 1, 3, 2, 4, 5)
    return updates.reshape(N_OWN, N_DP, CAPR, BS // 4, BS)
```

```python
import jax
import jax.numpy as jnp
from jax import lax
from jax.experimental import pallas as pl
from jax.experimental.pallas import tpu as pltpu
from jax.sharding import PartitionSpec as P

STAT_DECAY = 0.9
EPSILON = 1e-06
MESH = pl.DeviceIdType.MESH
BF = jnp.bfloat16
F32 = jnp.float32
NX, NY, NZ = 4, 8, 8
NE = 2 * NZ
BS = 512
TOK = 128
COLS = 960
HALF = 240
NB = 30
SLOTS = 64
NN = (((1,), (0,)), ((), ()))
NT = (((1,), (1,)), ((), ()))
TN = (((0,), (0,)), ((), ()))


def dot(a, b, dims=NN):
    return lax.dot_general(a, b, dims, preferred_element_type=F32)


def split(a):
    high = a.astype(BF)
    return high, (a - high.astype(F32)).astype(BF)


def exact_product(a, b):
    (ah, al), (bh, bl) = a, b
    return dot(ah, bh) + (dot(ah, bl) + dot(al, bh))


def wait(ref, sem):
    pltpu.make_async_copy(ref, ref, sem).wait()


def kernel(
    tab, acts, grads, stats, out,
    bt, am, part, snd, rcv, summed, tiles, outgoing, h4, rt, stat, work, res, got,
    b_send, b_recv, a_send, a_recv, f_send, f_recv, r_send, r_recv, t_send, t_recv,
    o_send, o_recv, h_send, h_recv, q_send, q_recv, u_send, u_recv, s_sem,
):
    own = lax.axis_index("own")
    dp = lax.axis_index("dp")
    y, x = lax.div(own, NX), lax.rem(own, NX)
    z, c = lax.div(dp, 2), lax.rem(dp, 2)
    brow, side = lax.div(z, 2), lax.rem(z, 2)
    sibling = (own, dp + 1 - 2 * c)
    pair = (own, dp + 2 - 4 * side)

    def ring(step):
        return lax.rem(y + step + NY, NY)

    def remote(src, dst, send_sem, recv_sem, device):
        return pltpu.make_async_remote_copy(
            src_ref=src, dst_ref=dst, send_sem=send_sem, recv_sem=recv_sem,
            device_id=device, device_id_type=MESH,
        )

    stat_copy = pltpu.make_async_copy(stats, stat, s_sem)
    stat_copy.start()

    barrier = pltpu.get_barrier_semaphore()

    def greet(device):
        pl.semaphore_signal(barrier, inc=1, device_id=device, device_id_type=MESH)

    for i in range(1, NX):
        greet((y * NX + lax.rem(x + i, NX), dp))
    greet((ring(1) * NX + x, dp))
    greet((ring(-1) * NX + x, dp))
    for i in range(1, NE):
        greet((own, lax.rem(dp + i, NE)))
    mine = brow == x

    for i in range(NX):
        for s in range(2):
            @pl.when(jnp.logical_not(jnp.logical_and(x == i, z == 2 * x + s)))
            def _():
                greet((y * NX + i, 2 * (2 * x + s) + c))

    turned = jnp.swapaxes(grads[...].astype(F32), 0, 1).astype(BF)
    turned = turned.reshape(NB, 2, 16, TOK)
    for h in range(2):
        bt[x, pl.ds(480 * h, 480), :] = turned[:, h].reshape(480, TOK)
    tiles[NB] = jnp.zeros((16, 128), BF)

    pl.semaphore_wait(barrier, (NX - 1) + 2 + (NE - 1) + NZ - mine.astype(jnp.int32))

    b_copies = []
    for i in range(1, NX):
        copy = remote(
            bt.at[x], bt.at[x], b_send.at[i - 1], b_recv.at[x],
            (y * NX + lax.rem(x + i, NX), dp),
        )
        copy.start()
        b_copies.append(copy)

    for i in range(NZ):
        here = jnp.logical_and(mine, z == i)

        @pl.when(here)
        def _():
            pltpu.make_async_copy(acts, am.at[x, side, c], a_recv).start()

        @pl.when(jnp.logical_not(here))
        def _():
            remote(
                acts, am.at[x, side, c], a_send, a_recv, (y * NX + brow, 2 * i + c)
            ).start()

    wait(am.at[:, :, 0], a_recv)
    forward = remote(am.at[:, :, c], am.at[:, :, c], f_send, f_recv, sibling)
    forward.start()
    forward.wait_recv()
    for i in range(1, NX):
        other = lax.rem(x + i, NX)
        wait(bt.at[other], b_recv.at[other])

    right = jnp.concatenate(
        [
            jnp.concatenate([am[i, s, k] for s in range(2) for k in range(2)], axis=1)
            for i in range(NX)
        ],
        axis=0,
    )
    for h in range(2):
        left = jnp.concatenate([bt[i, pl.ds(480 * h, 480), :] for i in range(NX)], axis=1)
        product = dot(left, right)
        for k in range(4):
            part[4 * h + k] = product[:, 128 * k : 128 * k + 128]

    started = []

    def hop(way, step, half, fresh):
        sign = 1 - 2 * way
        piece = ring(sign * (4 - step))
        value = part[piece, pl.ds(HALF * half, HALF), :]
        if not fresh:
            wait(rcv.at[way, step - 1, half], r_recv.at[way, step - 1, half])
            value = value + rcv[way, step - 1, half].astype(F32)
        snd[way, step, half] = value.astype(BF)
        copy = remote(
            snd.at[way, step, half], rcv.at[way, step, half],
            r_send.at[way, step, half], r_recv.at[way, step, half],
            (ring(sign) * NX + x, dp),
        )
        copy.start()
        started.append(copy)

    for way in range(2):
        hop(way, 0, 1 - way, True)
    for way in range(2):
        hop(way, 1, way, True)
    for step in range(1, 4):
        for way in range(2):
            hop(way, step, 1 - way, False)
        if step < 3:
            for way in range(2):
                hop(way, step + 1, way, False)
    for half in range(2):
        value = part[y, pl.ds(HALF * half, HALF), :]
        for way in range(2):
            wait(rcv.at[way, 3, half], r_recv.at[way, 3, half])
            value = value + rcv[way, 3, half].astype(F32)
        summed[pl.ds(15 * half, 15)] = value.astype(BF).reshape(15, 16, 128)

    def spread(k, carry):
        place = NB * dp + k
        target = lax.rem(place, NE)
        block = lax.div(place, NE)

        @pl.when(target == dp)
        def _():
            pltpu.make_async_copy(summed.at[k], tiles.at[block], t_recv).start()

        @pl.when(target != dp)
        def _():
            remote(summed.at[k], tiles.at[block], t_send, t_recv, (own, target)).start()

        return carry

    lax.fori_loop(0, NB, spread, 0)
    wait(tiles.at[pl.ds(0, NB)], t_recv)

    lanes = pl.ds(pl.multiple_of(128 * lax.rem(y, 4), 128), 128)
    rows = pl.ds(pl.multiple_of(16 * lax.div(y, 4), 16), 16)

    def deliver(k, carry):
        owner, slot = lax.div(k, 2), lax.rem(k, 2)
        target = 2 * (2 * x + slot) + c
        outgoing[k] = tiles[tab[SLOTS * x + k]]
        here = jnp.logical_and(owner == own, target == dp)

        @pl.when(here)
        def _():
            pltpu.make_async_copy(outgoing.at[k], h4.at[z, c, rows, lanes], o_recv).start()

        @pl.when(jnp.logical_not(here))
        def _():
            remote(
                outgoing.at[k], h4.at[z, c, rows, lanes], o_send, o_recv, (owner, target)
            ).start()

        return carry

    lax.fori_loop(0, SLOTS, deliver, 0)
    wait(h4.at[:, 0], o_recv)
    swap = remote(h4.at[:, c], h4.at[:, c], h_send, h_recv, sibling)
    swap.start()
    stat_copy.wait()
    swap.wait_recv()

    block = h4[...].reshape(BS, BS)

    @pl.when(c == 0)
    def _():
        work[...] = dot(block, block, TN)

    @pl.when(c != 0)
    def _():
        work[...] = dot(block, block, NT)

    factor = STAT_DECAY * stat[...] + (1.0 - STAT_DECAY) * work[...]
    eye = lax.broadcasted_iota(jnp.int32, (BS, BS), 0) == lax.broadcasted_iota(
        jnp.int32, (BS, BS), 1
    )
    scale = jnp.sum(jnp.where(eye, factor, 0.0)) / BS + EPSILON
    first = (jnp.where(eye, 5.0, 0.0) - factor / scale) / 4.0
    pieces = split(first)
    square = exact_product(pieces, pieces)
    pieces = split(square)
    fourth = exact_product(pieces, pieces)
    moved = exact_product(split(fourth), split(5.0 * first - 4.0 * square))
    rt[c] = ((5.0 * first - moved) / 4.0).astype(BF)
    roots = remote(rt.at[c], rt.at[c], q_send, q_recv, sibling)
    roots.start()
    wide = block.astype(F32)
    grad_scale = jnp.sqrt(jnp.sum(wide * wide) / (BS * BS) + EPSILON)
    roots.wait_recv()

    carried = dot(rt[0], block, NT).astype(BF)
    whole = dot(carried, rt[1])
    prec_scale = jnp.sqrt(jnp.sum(whole * whole) / (BS * BS) + EPSILON)
    res[...] = (whole * (grad_scale / prec_scale)).astype(BF).reshape(4, 128, BS)
    last = remote(res.at[2 * (1 - side) + c], got, u_send, u_recv, pair)
    last.start()
    out[0, 0, side] = res[2 * side + c]
    last.wait_recv()
    out[0, 0, 1 - side] = got[...]

    last.wait_send()
    roots.wait_send()
    swap.wait_send()
    forward.wait_send()
    for copy in b_copies + started:
        copy.wait_send()

    @pl.when(mine)
    def _():
        wait(bt.at[0, pl.ds(0, 7 * 128)], a_send)
        wait(outgoing.at[pl.ds(0, SLOTS - 1)], o_send)

    @pl.when(jnp.logical_not(mine))
    def _():
        wait(am.at[:, :, 0], a_send)
        wait(outgoing, o_send)

    two = lax.rem(3 * dp, NE) < NB - NE

    @pl.when(two)
    def _():
        wait(summed.at[pl.ds(0, NB - 2)], t_send)

    @pl.when(jnp.logical_not(two))
    def _():
        wait(summed.at[pl.ds(0, NB - 1)], t_send)


def slot_table(owner, col_index):
    owners = owner[:, 0].reshape(col_index.shape)
    positions = jnp.arange(NB, dtype=jnp.int32)
    earlier = positions[None, :] < positions[:, None]
    same = owners[:, :, None] == owners[:, None, :]
    slot = jnp.sum((same & earlier[None]).astype(jnp.int32), axis=2)
    place = 2 * owners + slot
    hit = place[:, None, :] == jnp.arange(SLOTS, dtype=jnp.int32)[None, :, None]
    return (NB + jnp.sum(jnp.where(hit, col_index[:, None, :] - NB, 0), axis=2)).reshape(-1)


def shards(acts, grads_out, stats, owner, col_index):
    dma = pltpu.SemaphoreType.DMA
    vmem = pl.BlockSpec(memory_space=pltpu.VMEM)
    return pl.pallas_call(
        kernel,
        out_shape=jax.ShapeDtypeStruct((1, 1, 2, 128, BS), BF),
        in_specs=[
            pl.BlockSpec(memory_space=pltpu.SMEM), vmem, vmem, pl.BlockSpec(memory_space=pl.ANY)
        ],
        out_specs=vmem,
        scratch_shapes=[
            pltpu.VMEM((NX, COLS, TOK), BF),
            pltpu.VMEM((NX, 2, 2, TOK, 128), BF),
            pltpu.VMEM((NY, 2 * HALF, 128), F32),
            pltpu.VMEM((2, 4, 2, HALF, 128), BF),
            pltpu.VMEM((2, 4, 2, HALF, 128), BF),
            pltpu.VMEM((NB, 16, 128), BF),
            pltpu.VMEM((NB + 1, 16, 128), BF),
            pltpu.VMEM((SLOTS, 16, 128), BF),
            pltpu.VMEM((NZ, 2, 32, BS), BF),
            pltpu.VMEM((2, BS, BS), BF),
            pltpu.VMEM((BS, BS), F32),
            pltpu.VMEM((BS, BS), F32),
            pltpu.VMEM((4, 128, BS), BF),
            pltpu.VMEM((128, BS), BF),
            dma((NX - 1,)), dma((NX,)), dma(()), dma(()), dma(()), dma(()),
            dma((2, 4, 2)), dma((2, 4, 2)), dma(()), dma(()),
            dma(()), dma(()), dma(()), dma(()), dma(()), dma(()), dma(()), dma(()), dma(()),
        ],
        compiler_params=pltpu.CompilerParams(
            collective_id=0, has_side_effects=True, vmem_limit_bytes=48 * 1024 * 1024
        ),
    )(slot_table(owner, col_index), acts, grads_out, stats.reshape(BS, BS))


def solution(mesh):
    return jax.shard_map(
        shards,
        mesh=mesh,
        in_specs=(P("own", "dp"), P("own", "dp"), P("own", "dp", None, None, None), P(), P()),
        out_specs=P("own", "dp", None, None, None),
        check_vma=False,
    )
```

```python
import jax
import jax.numpy as jnp
from jax import lax
from jax.experimental import pallas as pl
from jax.experimental.pallas import tpu as pltpu
from jax.sharding import PartitionSpec as P

STAT_DECAY = 0.9
EPSILON = 1e-06
MESH = pl.DeviceIdType.MESH
BF = jnp.bfloat16
F32 = jnp.float32
NX, NY, NZ = 4, 8, 8
NE = 2 * NZ
BS = 512
TOK = 128
COLS = 960
HALF = 240
SUB = 80
HOPS = 42
NB = 30
SLOTS = 64
ORDER = sorted(
    ((i, k, s) for i in range(NY) for k in range(NX) for s in range(2)),
    key=lambda t: -min(t[0], NY - t[0]) - min(t[1], NX - t[1]),
)
NN = (((1,), (0,)), ((), ()))
NT = (((1,), (1,)), ((), ()))
TN = (((0,), (0,)), ((), ()))


def dot(a, b, dims=NN):
    return lax.dot_general(a, b, dims, preferred_element_type=F32)


def split(a):
    high = a.astype(BF)
    return high, (a - high.astype(F32)).astype(BF)


def exact_product(a, b):
    (ah, al), (bh, bl) = a, b
    return dot(ah, bh) + (dot(ah, bl) + dot(al, bh))


def wait(ref, sem):
    pltpu.make_async_copy(ref, ref, sem).wait()


def kernel(
    owner, col_index, acts, grads, stats, out,
    bt, am, part, snd, rcv, summed, tiles, outgoing, h4, rt, stat, work, res, got, slots, table,
    b_send, b_recv, a_send, a_recv, f_send, f_recv, r_send, r_recv, t_send, t_recv,
    o_send, o_recv, h_send, h_recv, q_send, q_recv, u_send, u_recv, s_sem, g_sem,
):
    own = lax.axis_index("own")
    dp = lax.axis_index("dp")
    y, x = lax.div(own, NX), lax.rem(own, NX)
    z, c = lax.div(dp, 2), lax.rem(dp, 2)
    side = lax.rem(z, 2)
    brow = lax.div(z, 2)
    crow = lax.rem(x + z, NX)
    mine = brow == crow
    spot = 2 * (4 * side + x) + c
    sibling = (own, dp + 1 - 2 * c)
    pair = (own, dp + 2 - 4 * side)

    def ring(step):
        return lax.rem(y + step + NY, NY)

    def remote(src, dst, send_sem, recv_sem, device):
        return pltpu.make_async_remote_copy(
            src_ref=src, dst_ref=dst, send_sem=send_sem, recv_sem=recv_sem,
            device_id=device, device_id_type=MESH,
        )

    pending = []

    stat_copy = pltpu.make_async_copy(stats, stat, s_sem)
    stat_copy.start()

    barrier = pltpu.get_barrier_semaphore()

    def greet(device):
        pl.semaphore_signal(barrier, inc=1, device_id=device, device_id_type=MESH)

    for i in (1, -1):
        greet((y * NX + lax.rem(x + i + NX, NX), dp))
        greet((ring(i) * NX + x, dp))
    greet(sibling)
    for i in range(NX):
        for s in range(2):
            @pl.when(jnp.logical_not(jnp.logical_and(x == i, z == 2 * crow + s)))
            def _():
                greet((y * NX + i, 2 * (2 * crow + s) + c))

    turned = grads[...].reshape(NB, 2, 16, TOK)
    for g in range(2):
        for h in range(2):
            bt[x, pl.ds(HALF * (2 * g + h), HALF), :] = turned[15 * g : 15 * g + 15, h].reshape(
                HALF, TOK
            )
    summed[...] = jnp.zeros_like(summed)
    tiles[2 * NE] = jnp.zeros((16, 128), BF)

    lane = lax.broadcasted_iota(jnp.int32, (8, 128), 1)
    none = jnp.full((8, 128), NB, jnp.int32)

    def enter(k, taken):
        hit = lane == owner[NB * brow + k]
        free = taken[0] == NB
        return (
            jnp.where(jnp.logical_and(hit, free), col_index[brow, k], taken[0]),
            jnp.where(jnp.logical_and(hit, jnp.logical_not(free)), col_index[brow, k], taken[1]),
        )

    for slot, taken in enumerate(lax.fori_loop(0, NB, enter, (none, none))):
        place = NE * taken + spot
        source = lax.shift_right_logical(place * 2185, 16)
        tile = 2 * source + lax.shift_right_logical(place - NB * source, 4)
        slots[slot] = jnp.where(taken == NB, 2 * NE, tile)
    table_copy = pltpu.make_async_copy(slots, table, g_sem)
    table_copy.start()

    pl.semaphore_wait(barrier, 5 + NZ - mine.astype(jnp.int32))

    for i in range(NZ):
        here = jnp.logical_and(mine, z == i)

        @pl.when(here)
        def _():
            pltpu.make_async_copy(acts, am.at[x, side, c], a_recv).start()

        @pl.when(jnp.logical_not(here))
        def _():
            remote(
                acts, am.at[x, side, c], a_send, a_recv,
                (y * NX + lax.rem(brow - i + 2 * NX, NX), 2 * i + c),
            ).start()

    @pending.append
    def _():
        @pl.when(mine)
        def _():
            wait(bt.at[0, pl.ds(0, 7 * 128)], a_send)

        @pl.when(jnp.logical_not(mine))
        def _():
            wait(am.at[:, :, 0], a_send)

    def pass_on(shard, g, way, kind):
        there = bt.at[shard, pl.ds(2 * HALF * g, 2 * HALF)]
        copy = remote(
            there, there, b_send.at[g, kind], b_recv.at[g, kind],
            (y * NX + lax.rem(x + (1 if way == 0 else NX - 1), NX), dp),
        )
        copy.start()
        pending.append(copy.wait_send)

    def arrive(g, kind):
        shard = lax.rem(x + (NX - 1, 1, 2)[kind], NX)
        wait(bt.at[shard, pl.ds(2 * HALF * g, 2 * HALF)], b_recv.at[g, kind])
        return shard

    for g in range(2):
        for way in range(2):
            pass_on(x, g, way, way)
    pass_on(arrive(0, 0), 0, 0, 2)
    pass_on(arrive(1, 1), 1, 1, 2)

    wait(am.at[:, :, 0], a_recv)
    forward = remote(am.at[:, :, c], am.at[:, :, c], f_send, f_recv, sibling)
    forward.start()
    pending.append(forward.wait_send)
    forward.wait_recv()
    arrive(0, 1)
    arrive(0, 2)

    right = jnp.concatenate(
        [
            jnp.concatenate([am[i, s, k] for s in range(2) for k in range(2)], axis=1)
            for i in range(NX)
        ],
        axis=0,
    )
    def multiply(g):
        for h in range(2):
            rows = pl.ds(HALF * (2 * g + h), HALF)
            left = jnp.concatenate([bt[i, rows, :] for i in range(NX)], axis=1)
            product = dot(left, right)
            for k in range(4):
                part[4 * h + k, pl.ds(HALF * g, HALF), :] = product[:, 128 * k : 128 * k + 128]

    where = {}
    for step in range(4):
        for way in range(2):
            for sub in range(6):
                if step or sub // 3 != way:
                    where[way, step, sub] = len(where)

    def hop(way, step, half, fresh):
        sign = 1 - 2 * way
        piece = ring(sign * (4 - step))
        for sub in range(3 * half, 3 * half + 3):
            value = part[piece, pl.ds(SUB * sub, SUB), :]
            if not fresh:
                last = where[way, step - 1, sub]
                wait(rcv.at[last], r_recv.at[last])
                value = value + rcv[last].astype(F32)
            now = where[way, step, sub]
            snd[now] = value.astype(BF)
            remote(
                snd.at[now], rcv.at[now], r_send, r_recv.at[now], (ring(sign) * NX + x, dp)
            ).start()

    multiply(0)
    hop(1, 0, 0, True)
    hop(0, 1, 0, True)
    arrive(1, 0)
    arrive(1, 2)
    multiply(1)
    hop(0, 0, 1, True)
    hop(1, 1, 1, True)
    for step in range(1, 4):
        for way in (1, 0):
            hop(way, step, 1 - way, False)
        if step < 3:
            for way in (0, 1):
                hop(way, step + 1, way, False)
    pending.append(lambda: wait(snd, r_send))
    for sub in range(6):
        value = part[y, pl.ds(SUB * sub, SUB), :]
        for way in range(2):
            last = where[way, 3, sub]
            wait(rcv.at[last], r_recv.at[last])
            value = value + rcv[last].astype(F32)
        value = value.astype(BF).reshape(5, 16, 128)
        for i in range(5):
            k = 5 * sub + i
            summed[lax.rem(NB * dp + k, NE), k // NE] = value[i]

    for i in (2, 1, 3, 0):
        for s in range(2):
            for k in range(2):
                column = lax.rem(x + i, NX)
                target = 2 * (2 * crow + s) + k
                tile = 2 * (4 * s + column) + k
                here = target == dp if i == 0 else False

                def local(tile=tile):
                    pltpu.make_async_copy(
                        summed.at[tile], tiles.at[pl.ds(2 * dp, 2)], t_recv
                    ).start()

                def away(tile=tile, column=column, target=target):
                    remote(
                        summed.at[tile], tiles.at[pl.ds(2 * dp, 2)], t_send, t_recv,
                        (y * NX + column, target),
                    ).start()

                if i == 0:
                    pl.when(here)(local)
                    pl.when(jnp.logical_not(here))(away)
                else:
                    away()

    @pending.append
    def _():
        @pl.when(mine)
        def _():
            wait(summed.at[pl.ds(0, NE - 1)], t_send)

        @pl.when(jnp.logical_not(mine))
        def _():
            wait(summed, t_send)

    wait(tiles.at[pl.ds(0, 2 * NE)], t_recv)

    lanes = pl.ds(pl.multiple_of(128 * lax.rem(y, 4), 128), 128)
    rows = pl.ds(pl.multiple_of(16 * lax.div(y, 4), 16), 16)

    here = h4.at[4 * side + x, c, rows, lanes]
    table_copy.wait()
    for count, (i, k, s) in enumerate(ORDER):
        held = ring(i) * NX + lax.rem(x + k, NX)
        target = 2 * (2 * brow + s) + c
        outgoing[count] = tiles[table[s, 0, held]]

        def local(count=count):
            pltpu.make_async_copy(outgoing.at[count], here, o_recv).start()

        def away(count=count, held=held, target=target):
            remote(outgoing.at[count], here, o_send, o_recv, (held, target)).start()

        if i == 0 and k == 0:
            pl.when(side == s)(local)
            pl.when(side != s)(away)
        else:
            away()

    pending.append(lambda: wait(outgoing.at[pl.ds(0, SLOTS - 1)], o_send))
    wait(h4.at[:, 0], o_recv)
    swap = remote(h4.at[:, c], h4.at[:, c], h_send, h_recv, sibling)
    swap.start()
    pending.append(swap.wait_send)
    stat_copy.wait()
    swap.wait_recv()

    block = h4[...].reshape(BS, BS)

    @pl.when(c == 0)
    def _():
        work[...] = dot(block, block, TN)

    @pl.when(c != 0)
    def _():
        work[...] = dot(block, block, NT)

    factor = STAT_DECAY * stat[...] + (1.0 - STAT_DECAY) * work[...]
    eye = lax.broadcasted_iota(jnp.int32, (BS, BS), 0) == lax.broadcasted_iota(
        jnp.int32, (BS, BS), 1
    )
    scale = jnp.sum(jnp.where(eye, factor, 0.0)) / BS + EPSILON
    first = (jnp.where(eye, 5.0, 0.0) - factor / scale) / 4.0
    pieces = split(first)
    square = exact_product(pieces, pieces)
    pieces = split(square)
    fourth = exact_product(pieces, pieces)
    moved = exact_product(split(fourth), split(5.0 * first - 4.0 * square))
    rt[c] = ((5.0 * first - moved) / 4.0).astype(BF)
    roots = remote(rt.at[c], rt.at[c], q_send, q_recv, sibling)
    roots.start()
    pending.append(roots.wait_send)
    wide = block.astype(F32)
    grad_scale = jnp.sqrt(jnp.sum(wide * wide) / (BS * BS) + EPSILON)
    roots.wait_recv()

    carried = dot(rt[0], block, NT).astype(BF)
    whole = dot(carried, rt[1])
    prec_scale = jnp.sqrt(jnp.sum(whole * whole) / (BS * BS) + EPSILON)
    res[...] = (whole * (grad_scale / prec_scale)).astype(BF).reshape(4, 128, BS)
    last = remote(res.at[2 * (1 - side) + c], got, u_send, u_recv, pair)
    last.start()
    pending.append(last.wait_send)
    out[0, 0, side] = res[2 * side + c]
    last.wait_recv()
    out[0, 0, 1 - side] = got[...]

    for done in pending:
        done()


def shards(acts, grads_out, stats, owner, col_index):
    dma = pltpu.SemaphoreType.DMA
    smem = pl.BlockSpec(memory_space=pltpu.SMEM)
    vmem = pl.BlockSpec(memory_space=pltpu.VMEM)
    return pl.pallas_call(
        kernel,
        out_shape=jax.ShapeDtypeStruct((1, 1, 2, 128, BS), BF),
        in_specs=[
            smem, smem, vmem, vmem, pl.BlockSpec(memory_space=pl.ANY)
        ],
        out_specs=vmem,
        scratch_shapes=[
            pltpu.VMEM((NX, COLS, TOK), BF),
            pltpu.VMEM((NX, 2, 2, TOK, 128), BF),
            pltpu.VMEM((NY, 2 * HALF, 128), F32),
            pltpu.VMEM((HOPS, SUB, 128), BF),
            pltpu.VMEM((HOPS, SUB, 128), BF),
            pltpu.VMEM((NE, 2, 16, 128), BF),
            pltpu.VMEM((2 * NE + 1, 16, 128), BF),
            pltpu.VMEM((SLOTS, 16, 128), BF),
            pltpu.VMEM((NZ, 2, 32, BS), BF),
            pltpu.VMEM((2, BS, BS), BF),
            pltpu.VMEM((BS, BS), F32),
            pltpu.VMEM((BS, BS), F32),
            pltpu.VMEM((4, 128, BS), BF),
            pltpu.VMEM((128, BS), BF),
            pltpu.VMEM((2, 8, 128), jnp.int32),
            pltpu.SMEM((2, 8, 128), jnp.int32),
            dma((2, 3)), dma((2, 3)), dma(()), dma(()), dma(()), dma(()),
            dma(()), dma((HOPS,)), dma(()), dma(()),
            dma(()), dma(()), dma(()), dma(()), dma(()), dma(()), dma(()), dma(()), dma(()), dma(()),
        ],
        compiler_params=pltpu.CompilerParams(
            collective_id=0, has_side_effects=True, vmem_limit_bytes=60 * 1024 * 1024
        ),
    )(owner.reshape(-1), col_index, acts, grads_out.T, stats.reshape(BS, BS))


def solution(mesh):
    return jax.shard_map(
        shards,
        mesh=mesh,
        in_specs=(P("own", "dp"), P("own", "dp"), P("own", "dp", None, None, None), P(), P()),
        out_specs=P("own", "dp", None, None, None),
        check_vma=False,
    )
```

```python
import jax
import jax.numpy as jnp
from jax import lax
from jax.experimental import pallas as pl
from jax.experimental.pallas import tpu as pltpu
from jax.sharding import PartitionSpec as P

STAT_DECAY = 0.9
EPSILON = 1e-06
MESH = pl.DeviceIdType.MESH
BF = jnp.bfloat16
F32 = jnp.float32
NX, NY, NZ = 4, 8, 8
NE = 2 * NZ
BS = 512
TOK = 128
HALF = 240
SUB = 80
HOPS = 42
NB = 30
SLOTS = 64
ORDER = sorted(
    ((i, k, s) for i in range(NY) for k in range(NX) for s in range(2)),
    key=lambda t: -min(t[0], NY - t[0]) - min(t[1], NX - t[1]),
)
NN = (((1,), (0,)), ((), ()))
NT = (((1,), (1,)), ((), ()))
TN = (((0,), (0,)), ((), ()))


def dot(a, b, dims=NN):
    return lax.dot_general(a, b, dims, preferred_element_type=F32)


def split(a):
    high = a.astype(BF)
    return high, (a - high.astype(F32)).astype(BF)


def exact_product(a, b):
    (ah, al), (bh, bl) = a, b
    return dot(ah, bh) + (dot(ah, bl) + dot(al, bh))


def wait(ref, sem):
    pltpu.make_async_copy(ref, ref, sem).wait()


def kernel(
    owner, col_index, acts, grads, stats, out,
    ax, bt, am, part, snd, rcv, summed, tiles, outgoing, h4, rt, stat, work, res, slots, table,
    b_send, b_recv, a_send, a_recv, f_send, f_recv, r_send, r_recv, t_send, t_recv,
    o_send, o_recv, h_send, h_recv, q_send, q_recv, u_send, u_recv, s_sem, g_sem, i_sem, w_sem, know,
):
    own = lax.axis_index("own")
    dp = lax.axis_index("dp")
    y, x = lax.div(own, NX), lax.rem(own, NX)
    z, c = lax.div(dp, 2), lax.rem(dp, 2)
    side = lax.rem(z, 2)
    brow = lax.div(z, 2)
    crow = lax.rem(x + z, NX)
    mine = brow == crow
    spot = 2 * (4 * side + x) + c
    sibling = (own, dp + 1 - 2 * c)
    pair = (own, dp + 2 - 4 * side)

    def ring(step):
        return lax.rem(y + step + NY, NY)

    def remote(src, dst, send_sem, recv_sem, device):
        return pltpu.make_async_remote_copy(
            src_ref=src, dst_ref=dst, send_sem=send_sem, recv_sem=recv_sem,
            device_id=device, device_id_type=MESH,
        )

    pending = []

    barrier = pltpu.get_barrier_semaphore()

    def say(sem, device):
        pl.semaphore_signal(sem, inc=1, device_id=device, device_id_type=MESH)

    def along_x(step):
        return (y * NX + lax.rem(x + step + NX, NX), dp)

    def along_z(step):
        return (own, 2 * lax.rem(z + step + NZ, NZ) + c)

    for i in (1, 2, 3):
        say(barrier, along_x(i))
    for i in (1, -1):
        say(barrier, (ring(i) * NX + x, dp))
        for k in range(NX):
            say(barrier, (along_x(k)[0], along_z(i)[1]))
    say(barrier, sibling)

    acts_copy = pltpu.make_async_copy(acts, ax, i_sem.at[4])
    acts_copy.start()
    grads_copies = [
        pltpu.make_async_copy(
            grads.at[pl.ds(15 * g, 15), h], bt.at[x, pl.ds(15 * (2 * g + h), 15)],
            i_sem.at[2 * g + h],
        )
        for g in range(2)
        for h in range(2)
    ]
    for copy in grads_copies:
        copy.start()
    stat_copy = pltpu.make_async_copy(stats, stat, s_sem)
    stat_copy.start()
    summed[...] = jnp.zeros_like(summed)
    tiles[2 * NE] = jnp.zeros((16, 128), BF)

    lane = lax.broadcasted_iota(jnp.int32, (8, 128), 1)
    none = jnp.full((8, 128), NB, jnp.int32)

    def enter(k, taken):
        hit = lane == owner[NB * brow + k]
        free = taken[0] == NB
        return (
            jnp.where(jnp.logical_and(hit, free), col_index[brow, k], taken[0]),
            jnp.where(jnp.logical_and(hit, jnp.logical_not(free)), col_index[brow, k], taken[1]),
        )

    for slot, taken in enumerate(lax.fori_loop(0, NB, enter, (none, none))):
        place = NE * taken + spot
        source = lax.shift_right_logical(place * 2185, 16)
        tile = 2 * source + lax.shift_right_logical(place - NB * source, 4)
        slots[slot] = jnp.where(taken == NB, 2 * NE, tile)
    table_copy = pltpu.make_async_copy(slots, table, g_sem)
    table_copy.start()

    acts_copy.wait()
    for copy in grads_copies:
        copy.wait()
    pl.semaphore_wait(barrier, 14)
    for i in (1, -1):
        say(know.at[0], along_z(i))

    def pass_on(shard, g, way, kind):
        there = bt.at[shard, pl.ds(30 * g, 30)]
        copy = remote(
            there, there, b_send.at[g, kind], b_recv.at[g, kind], along_x(1 - 2 * way)
        )
        copy.start()
        pending.append(copy.wait_send)

    def arrive(g, kind):
        shard = lax.rem(x + (NX - 1, 1, 2)[kind], NX)
        wait(bt.at[shard, pl.ds(30 * g, 30)], b_recv.at[g, kind])
        return shard

    for g in range(2):
        for way in range(2):
            pass_on(x, g, way, way)

    pl.semaphore_wait(know.at[0], 2)
    for i in (2, -2):
        say(know.at[1], along_z(i))
    pl.semaphore_wait(know.at[1], 2)
    for i in (4, 3, 5, 2, 6, 1, 7, 0):
        plane = lax.rem(z + i, NZ)
        column = lax.rem(brow - plane + 2 * NX, NX)

        def local():
            pltpu.make_async_copy(ax, am.at[x, side, c], a_recv).start()

        def away(plane=plane, column=column):
            remote(
                ax, am.at[x, side, c], a_send, a_recv, (y * NX + column, 2 * plane + c)
            ).start()

        if i == 0:
            pl.when(mine)(local)
            pl.when(jnp.logical_not(mine))(away)
        else:
            away()
    pass_on(arrive(0, 0), 0, 0, 2)
    pass_on(arrive(1, 1), 1, 1, 2)

    @pending.append
    def _():
        @pl.when(mine)
        def _():
            wait(bt.at[0, pl.ds(0, 56)], a_send)

        @pl.when(jnp.logical_not(mine))
        def _():
            wait(am.at[:, :, 0], a_send)

    wait(am.at[:, :, 0], a_recv)
    forward = remote(am.at[:, :, c], am.at[:, :, c], f_send, f_recv, sibling)
    forward.start()
    pending.append(forward.wait_send)
    arrive(0, 1)
    arrive(0, 2)
    forward.wait_recv()

    right = jnp.concatenate(
        [
            jnp.concatenate([am[i, s, k] for s in range(2) for k in range(2)], axis=1)
            for i in range(NX)
        ],
        axis=0,
    )
    def multiply(g):
        for h in range(2):
            rows = pl.ds(15 * (2 * g + h), 15)
            left = jnp.concatenate(
                [bt[i, rows].reshape(HALF, TOK) for i in range(NX)], axis=1
            )
            product = dot(left, right)
            for k in range(4):
                part[4 * h + k, pl.ds(HALF * g, HALF), :] = product[:, 128 * k : 128 * k + 128]

    where = {}
    for step in range(4):
        for way in range(2):
            for sub in range(6):
                if step or sub // 3 != way:
                    where[way, step, sub] = len(where)

    def hop(way, step, half, fresh):
        sign = 1 - 2 * way
        piece = ring(sign * (4 - step))
        for sub in range(3 * half, 3 * half + 3):
            value = part[piece, pl.ds(SUB * sub, SUB), :]
            if not fresh:
                last = where[way, step - 1, sub]
                wait(rcv.at[last], r_recv.at[last])
                value = value + rcv[last].astype(F32)
            now = where[way, step, sub]
            snd[now] = value.astype(BF)
            remote(
                snd.at[now], rcv.at[now], r_send, r_recv.at[now], (ring(sign) * NX + x, dp)
            ).start()

    multiply(0)
    hop(1, 0, 0, True)
    hop(0, 1, 0, True)
    arrive(1, 0)
    arrive(1, 2)
    multiply(1)
    hop(0, 0, 1, True)
    hop(1, 1, 1, True)
    for step in range(1, 4):
        for way in (1, 0):
            hop(way, step, 1 - way, False)
        if step < 3:
            for way in (0, 1):
                hop(way, step + 1, way, False)
    pending.append(lambda: wait(snd, r_send))
    for sub in range(6):
        value = part[y, pl.ds(SUB * sub, SUB), :]
        for way in range(2):
            last = where[way, 3, sub]
            wait(rcv.at[last], r_recv.at[last])
            value = value + rcv[last].astype(F32)
        value = value.astype(BF).reshape(5, 16, 128)
        for i in range(5):
            k = 5 * sub + i
            summed[lax.rem(NB * dp + k, NE), k // NE] = value[i]

    for i in (2, 1, 3, 0):
        for s in range(2):
            for k in range(2):
                column = lax.rem(x + i, NX)
                target = 2 * (2 * crow + s) + k
                tile = 2 * (4 * s + column) + k
                here = target == dp if i == 0 else False

                def local(tile=tile):
                    pltpu.make_async_copy(
                        summed.at[tile], tiles.at[pl.ds(2 * dp, 2)], t_recv
                    ).start()

                def away(tile=tile, column=column, target=target):
                    remote(
                        summed.at[tile], tiles.at[pl.ds(2 * dp, 2)], t_send, t_recv,
                        (y * NX + column, target),
                    ).start()

                if i == 0:
                    pl.when(here)(local)
                    pl.when(jnp.logical_not(here))(away)
                else:
                    away()

    @pending.append
    def _():
        @pl.when(mine)
        def _():
            wait(summed.at[pl.ds(0, NE - 1)], t_send)

        @pl.when(jnp.logical_not(mine))
        def _():
            wait(summed, t_send)

    wait(tiles.at[pl.ds(0, 2 * NE)], t_recv)

    lanes = pl.ds(pl.multiple_of(128 * lax.rem(y, 4), 128), 128)
    rows = pl.ds(pl.multiple_of(16 * lax.div(y, 4), 16), 16)

    here = h4.at[4 * side + x, c, rows, lanes]
    table_copy.wait()
    for count, (i, k, s) in enumerate(ORDER):
        held = ring(i) * NX + lax.rem(x + k, NX)
        target = 2 * (2 * brow + s) + c
        outgoing[count] = tiles[table[s, 0, held]]

        def local(count=count):
            pltpu.make_async_copy(outgoing.at[count], here, o_recv).start()

        def away(count=count, held=held, target=target):
            remote(outgoing.at[count], here, o_send, o_recv, (held, target)).start()

        if i == 0 and k == 0:
            pl.when(side == s)(local)
            pl.when(side != s)(away)
        else:
            away()

    pending.append(lambda: wait(outgoing.at[pl.ds(0, SLOTS - 1)], o_send))
    wait(h4.at[:, 0], o_recv)
    swap = remote(h4.at[:, c], h4.at[:, c], h_send, h_recv, sibling)
    swap.start()
    pending.append(swap.wait_send)
    stat_copy.wait()
    swap.wait_recv()

    block = h4[...].reshape(BS, BS)

    @pl.when(c == 0)
    def _():
        work[...] = dot(block, block, TN)

    @pl.when(c != 0)
    def _():
        work[...] = dot(block, block, NT)

    factor = STAT_DECAY * stat[...] + (1.0 - STAT_DECAY) * work[...]
    eye = lax.broadcasted_iota(jnp.int32, (BS, BS), 0) == lax.broadcasted_iota(
        jnp.int32, (BS, BS), 1
    )
    scale = jnp.sum(jnp.where(eye, factor, 0.0)) / BS + EPSILON
    first = (jnp.where(eye, 5.0, 0.0) - factor / scale) / 4.0
    pieces = split(first)
    square = exact_product(pieces, pieces)
    pieces = split(square)
    fourth = exact_product(pieces, pieces)
    moved = exact_product(split(fourth), split(5.0 * first - 4.0 * square))
    rt[c] = ((5.0 * first - moved) / 4.0).astype(BF)
    roots = remote(rt.at[c], rt.at[c], q_send, q_recv, sibling)
    roots.start()
    pending.append(roots.wait_send)
    wide = block.astype(F32)
    grad_scale = jnp.sqrt(jnp.sum(wide * wide) / (BS * BS) + EPSILON)
    roots.wait_recv()

    carried = dot(rt[0], block, NT).astype(BF)
    whole = dot(carried, rt[1])
    prec_scale = jnp.sqrt(jnp.sum(whole * whole) / (BS * BS) + EPSILON)
    res[...] = (whole * (grad_scale / prec_scale)).astype(BF).reshape(4, 128, BS)
    keep = pltpu.make_async_copy(res.at[2 * side + c], out.at[0, 0, side], w_sem)
    last = remote(res.at[2 * (1 - side) + c], out.at[0, 0, side], u_send, u_recv, pair)
    last.start()
    keep.start()
    pending.append(last.wait_send)
    pending.append(keep.wait)
    last.wait_recv()

    for done in pending:
        done()


def shards(acts, grads_out, stats, owner, col_index):
    dma = pltpu.SemaphoreType.DMA
    smem = pl.BlockSpec(memory_space=pltpu.SMEM)
    hbm = pl.BlockSpec(memory_space=pl.ANY)
    return pl.pallas_call(
        kernel,
        out_shape=jax.ShapeDtypeStruct((1, 1, 2, 128, BS), BF),
        in_specs=[
            smem, smem, hbm, hbm, hbm
        ],
        out_specs=hbm,
        scratch_shapes=[
            pltpu.VMEM((TOK, 128), BF),
            pltpu.VMEM((NX, 2 * NB, 16, TOK), BF),
            pltpu.VMEM((NX, 2, 2, TOK, 128), BF),
            pltpu.VMEM((NY, 2 * HALF, 128), F32),
            pltpu.VMEM((HOPS, SUB, 128), BF),
            pltpu.VMEM((HOPS, SUB, 128), BF),
            pltpu.VMEM((NE, 2, 16, 128), BF),
            pltpu.VMEM((2 * NE + 1, 16, 128), BF),
            pltpu.VMEM((SLOTS, 16, 128), BF),
            pltpu.VMEM((NZ, 2, 32, BS), BF),
            pltpu.VMEM((2, BS, BS), BF),
            pltpu.VMEM((BS, BS), F32),
            pltpu.VMEM((BS, BS), F32),
            pltpu.VMEM((4, 128, BS), BF),
            pltpu.VMEM((2, 8, 128), jnp.int32),
            pltpu.SMEM((2, 8, 128), jnp.int32),
            dma((2, 3)), dma((2, 3)), dma(()), dma(()), dma(()), dma(()),
            dma(()), dma((HOPS,)), dma(()), dma(()),
            dma(()), dma(()), dma(()), dma(()), dma(()), dma(()), dma(()), dma(()), dma(()), dma(()),
            dma((5,)), dma(()), pltpu.SemaphoreType.REGULAR((2,)),
        ],
        compiler_params=pltpu.CompilerParams(
            collective_id=0, has_side_effects=True, vmem_limit_bytes=60 * 1024 * 1024
        ),
    )(owner.reshape(-1), col_index, acts, grads_out.T.reshape(NB, 2, 16, TOK), stats.reshape(BS, BS))


def solution(mesh):
    return jax.shard_map(
        shards,
        mesh=mesh,
        in_specs=(P("own", "dp"), P("own", "dp"), P("own", "dp", None, None, None), P(), P()),
        out_specs=P("own", "dp", None, None, None),
        check_vma=False,
    )
```

```python
import jax
import jax.numpy as jnp
from jax import lax
from jax.experimental import pallas as pl
from jax.experimental.pallas import tpu as pltpu
from jax.sharding import PartitionSpec as P

STAT_DECAY = 0.9
EPSILON = 1e-06
MESH = pl.DeviceIdType.MESH
BF = jnp.bfloat16
F32 = jnp.float32
NX, NY, NZ = 4, 8, 8
NE = 2 * NZ
BS = 512
TOK = 128
HALF = 240
SUB = 80
HOPS = 42
NB = 30
SLOTS = 64
ORDER = sorted(
    ((i, k, s) for i in range(NY) for k in range(NX) for s in range(2)),
    key=lambda t: -min(t[0], NY - t[0]) - min(t[1], NX - t[1]),
)
NN = (((1,), (0,)), ((), ()))
NT = (((1,), (1,)), ((), ()))
TN = (((0,), (0,)), ((), ()))


def dot(a, b, dims=NN):
    return lax.dot_general(a, b, dims, preferred_element_type=F32)


def wait(ref, sem):
    pltpu.make_async_copy(ref, ref, sem).wait()


def kernel(
    owner, col_index, acts, grads, stats, out,
    ax, bt, am, part, snd, rcv, summed, tiles, outgoing, h4, rt, stat, work, res, slots, table,
    b_send, b_recv, a_send, a_recv, f_send, f_recv, r_send, r_recv, t_send, t_recv,
    o_send, o_recv, h_send, h_recv, q_send, q_recv, u_send, u_recv, s_sem, g_sem, i_sem, w_sem, know,
):
    own = lax.axis_index("own")
    dp = lax.axis_index("dp")
    y, x = lax.div(own, NX), lax.rem(own, NX)
    z, c = lax.div(dp, 2), lax.rem(dp, 2)
    side = lax.rem(z, 2)
    brow = lax.div(z, 2)
    crow = lax.rem(x + z, NX)
    mine = brow == crow
    spot = 2 * (4 * side + x) + c
    sibling = (own, dp + 1 - 2 * c)
    pair = (own, dp + 2 - 4 * side)

    def ring(step):
        return lax.rem(y + step + NY, NY)

    def remote(src, dst, send_sem, recv_sem, device):
        return pltpu.make_async_remote_copy(
            src_ref=src, dst_ref=dst, send_sem=send_sem, recv_sem=recv_sem,
            device_id=device, device_id_type=MESH,
        )

    pending = []

    barrier = pltpu.get_barrier_semaphore()

    def say(sem, device):
        pl.semaphore_signal(sem, inc=1, device_id=device, device_id_type=MESH)

    def along_x(step):
        return (y * NX + lax.rem(x + step + NX, NX), dp)

    def along_z(step):
        return (own, 2 * lax.rem(z + step + NZ, NZ) + c)

    for i in (1, 2, 3):
        say(barrier, along_x(i))
    for i in (1, -1):
        say(barrier, (ring(i) * NX + x, dp))
        for k in range(NX):
            say(barrier, (along_x(k)[0], along_z(i)[1]))
            say(barrier, (along_x(k)[0], along_z(2 * i)[1]))
    say(barrier, sibling)

    acts_copy = pltpu.make_async_copy(acts, ax, i_sem.at[4])
    acts_copy.start()
    grads_copies = [
        pltpu.make_async_copy(
            grads.at[pl.ds(15 * g, 15), h], bt.at[x, pl.ds(15 * (2 * g + h), 15)],
            i_sem.at[2 * g + h],
        )
        for g in range(2)
        for h in range(2)
    ]
    for copy in grads_copies:
        copy.start()
    stat_copy = pltpu.make_async_copy(stats, stat, s_sem)
    stat_copy.start()
    summed[...] = jnp.zeros_like(summed)
    tiles[2 * NE] = jnp.zeros((16, 128), BF)

    lane = lax.broadcasted_iota(jnp.int32, (8, 128), 1)
    none = jnp.full((8, 128), NB, jnp.int32)

    def enter(k, taken):
        hit = lane == owner[NB * brow + k]
        free = taken[0] == NB
        return (
            jnp.where(jnp.logical_and(hit, free), col_index[brow, k], taken[0]),
            jnp.where(jnp.logical_and(hit, jnp.logical_not(free)), col_index[brow, k], taken[1]),
        )

    for slot, taken in enumerate(lax.fori_loop(0, NB, enter, (none, none))):
        place = NE * taken + spot
        source = lax.shift_right_logical(place * 2185, 16)
        tile = 2 * source + lax.shift_right_logical(place - NB * source, 4)
        slots[slot] = jnp.where(taken == NB, 2 * NE, tile)
    table_copy = pltpu.make_async_copy(slots, table, g_sem)
    table_copy.start()

    acts_copy.wait()
    for copy in grads_copies:
        copy.wait()
    pl.semaphore_wait(barrier, 22)
    for i in (2, -2):
        say(know, along_z(i))

    def pass_on(shard, g, way, kind):
        there = bt.at[shard, pl.ds(30 * g, 30)]
        copy = remote(
            there, there, b_send.at[g, kind], b_recv.at[g, kind], along_x(1 - 2 * way)
        )
        copy.start()
        pending.append(copy.wait_send)

    def arrive(g, kind):
        shard = lax.rem(x + (NX - 1, 1, 2)[kind], NX)
        wait(bt.at[shard, pl.ds(30 * g, 30)], b_recv.at[g, kind])
        return shard

    for g in range(2):
        for way in range(2):
            pass_on(x, g, way, way)

    pl.semaphore_wait(know, 2)
    for i in (4, 3, 5, 2, 6, 1, 7, 0):
        plane = lax.rem(z + i, NZ)
        column = lax.rem(brow - plane + 2 * NX, NX)

        def local():
            pltpu.make_async_copy(ax, am.at[x, side, c], a_recv.at[side]).start()

        def away(plane=plane, column=column):
            remote(
                ax, am.at[x, side, c], a_send, a_recv.at[side], (y * NX + column, 2 * plane + c)
            ).start()

        if i == 0:
            pl.when(mine)(local)
            pl.when(jnp.logical_not(mine))(away)
        else:
            away()
    pass_on(arrive(0, 0), 0, 0, 2)
    pass_on(arrive(1, 1), 1, 1, 2)

    @pending.append
    def _():
        @pl.when(mine)
        def _():
            wait(bt.at[0, pl.ds(0, 56)], a_send)

        @pl.when(jnp.logical_not(mine))
        def _():
            wait(am.at[:, :, 0], a_send)

    forwards = []
    for s in range(2):
        wait(am.at[:, s, c], a_recv.at[s])
        forwards.append(
            remote(am.at[:, s, c], am.at[:, s, c], f_send.at[s], f_recv.at[s], sibling)
        )
        forwards[s].start()
        pending.append(forwards[s].wait_send)
    arrive(0, 1)
    arrive(0, 2)
    for copy in forwards:
        copy.wait_recv()

    right = jnp.concatenate(
        [
            jnp.concatenate([am[i, s, k] for s in range(2) for k in range(2)], axis=1)
            for i in range(NX)
        ],
        axis=0,
    )
    def multiply(g):
        for h in range(2):
            rows = pl.ds(15 * (2 * g + h), 15)
            left = jnp.concatenate(
                [bt[i, rows].reshape(HALF, TOK) for i in range(NX)], axis=1
            )
            product = dot(left, right)
            for k in range(4):
                part[4 * h + k, pl.ds(HALF * g, HALF), :] = product[:, 128 * k : 128 * k + 128]

    where = {}
    for step in range(4):
        for way in range(2):
            for sub in range(6):
                if step or sub // 3 != way:
                    where[way, step, sub] = len(where)

    def hop(way, step, half, fresh):
        sign = 1 - 2 * way
        piece = ring(sign * (4 - step))
        for sub in range(3 * half, 3 * half + 3):
            value = part[piece, pl.ds(SUB * sub, SUB), :]
            if not fresh:
                last = where[way, step - 1, sub]
                wait(rcv.at[last], r_recv.at[last])
                value = value + rcv[last].astype(F32)
            now = where[way, step, sub]
            snd[now] = value.astype(BF)
            remote(
                snd.at[now], rcv.at[now], r_send, r_recv.at[now], (ring(sign) * NX + x, dp)
            ).start()

    multiply(0)
    hop(1, 0, 0, True)
    hop(0, 1, 0, True)
    arrive(1, 0)
    arrive(1, 2)
    multiply(1)
    hop(0, 0, 1, True)
    hop(1, 1, 1, True)
    for step in range(1, 4):
        for way in (1, 0):
            hop(way, step, 1 - way, False)
        if step < 3:
            for way in (0, 1):
                hop(way, step + 1, way, False)
    pending.append(lambda: wait(snd, r_send))
    for sub in range(6):
        value = part[y, pl.ds(SUB * sub, SUB), :]
        for way in range(2):
            last = where[way, 3, sub]
            wait(rcv.at[last], r_recv.at[last])
            value = value + rcv[last].astype(F32)
        value = value.astype(BF).reshape(5, 16, 128)
        for i in range(5):
            k = 5 * sub + i
            summed[lax.rem(NB * dp + k, NE), k // NE] = value[i]

    for i in (2, 1, 3, 0):
        for s in range(2):
            for k in range(2):
                column = lax.rem(x + i, NX)
                target = 2 * (2 * crow + s) + k
                tile = 2 * (4 * s + column) + k
                here = target == dp if i == 0 else False

                def local(tile=tile):
                    pltpu.make_async_copy(
                        summed.at[tile], tiles.at[pl.ds(2 * dp, 2)], t_recv
                    ).start()

                def away(tile=tile, column=column, target=target):
                    remote(
                        summed.at[tile], tiles.at[pl.ds(2 * dp, 2)], t_send, t_recv,
                        (y * NX + column, target),
                    ).start()

                if i == 0:
                    pl.when(here)(local)
                    pl.when(jnp.logical_not(here))(away)
                else:
                    away()

    @pending.append
    def _():
        @pl.when(mine)
        def _():
            wait(summed.at[pl.ds(0, NE - 1)], t_send)

        @pl.when(jnp.logical_not(mine))
        def _():
            wait(summed, t_send)

    wait(tiles.at[pl.ds(0, 2 * NE)], t_recv)

    lanes = pl.ds(pl.multiple_of(128 * lax.rem(y, 4), 128), 128)
    rows = pl.ds(pl.multiple_of(16 * lax.div(y, 4), 16), 16)

    here = h4.at[4 * side + x, c, rows, lanes]
    table_copy.wait()
    for count, (i, k, s) in enumerate(ORDER):
        held = ring(i) * NX + lax.rem(x + k, NX)
        target = 2 * (2 * brow + s) + c
        outgoing[count] = tiles[table[s, 0, held]]

        def local(count=count):
            pltpu.make_async_copy(outgoing.at[count], here, o_recv).start()

        def away(count=count, held=held, target=target):
            remote(outgoing.at[count], here, o_send, o_recv, (held, target)).start()

        if i == 0 and k == 0:
            pl.when(side == s)(local)
            pl.when(side != s)(away)
        else:
            away()

    pending.append(lambda: wait(outgoing.at[pl.ds(0, SLOTS - 1)], o_send))
    wait(h4.at[:, 0], o_recv)
    swap = remote(h4.at[:, c], h4.at[:, c], h_send, h_recv, sibling)
    swap.start()
    pending.append(swap.wait_send)
    stat_copy.wait()
    swap.wait_recv()

    block = h4[...].reshape(BS, BS)

    @pl.when(c == 0)
    def _():
        work[...] = dot(block, block, TN)

    @pl.when(c != 0)
    def _():
        work[...] = dot(block, block, NT)

    factor = STAT_DECAY * stat[...] + (1.0 - STAT_DECAY) * work[...]
    eye = lax.broadcasted_iota(jnp.int32, (BS, BS), 0) == lax.broadcasted_iota(
        jnp.int32, (BS, BS), 1
    )
    scale = jnp.sum(jnp.where(eye, factor, 0.0)) / BS + EPSILON
    first = (jnp.where(eye, 5.0, 0.0) - factor / scale) / 4.0
    near = first.astype(BF)
    square = dot(near, near)
    rest = (5.0 * near.astype(F32) - 4.0 * square).astype(BF)
    square = square.astype(BF)
    fourth = dot(square, square).astype(BF)
    roots = []
    for k in range(2):
        rows = slice(BS // 2 * k, BS // 2 * k + BS // 2)
        moved = dot(fourth[rows], rest)
        there = rt.at[c, pl.ds(BS // 2 * k, BS // 2)]
        rt[c, pl.ds(BS // 2 * k, BS // 2), :] = ((5.0 * first[rows] - moved) / 4.0).astype(BF)
        roots.append(remote(there, there, q_send.at[k], q_recv.at[k], sibling))
        roots[k].start()
        pending.append(roots[k].wait_send)
    wide = block.astype(F32)
    grad_scale = jnp.sqrt(jnp.sum(wide * wide) / (BS * BS) + EPSILON)
    for copy in roots:
        copy.wait_recv()

    carried = dot(rt[0], block, NT).astype(BF)
    whole = dot(carried, rt[1])
    prec_scale = jnp.sqrt(jnp.sum(whole * whole) / (BS * BS) + EPSILON)
    res[...] = (whole * (grad_scale / prec_scale)).astype(BF).reshape(4, 128, BS)
    keep = pltpu.make_async_copy(res.at[2 * side + c], out.at[0, 0, side], w_sem)
    last = remote(res.at[2 * (1 - side) + c], out.at[0, 0, side], u_send, u_recv, pair)
    last.start()
    keep.start()
    pending.append(last.wait_send)
    pending.append(keep.wait)
    last.wait_recv()

    for done in pending:
        done()


def shards(acts, grads_out, stats, owner, col_index):
    dma = pltpu.SemaphoreType.DMA
    smem = pl.BlockSpec(memory_space=pltpu.SMEM)
    hbm = pl.BlockSpec(memory_space=pl.ANY)
    return pl.pallas_call(
        kernel,
        out_shape=jax.ShapeDtypeStruct((1, 1, 2, 128, BS), BF),
        in_specs=[
            smem, smem, hbm, hbm, hbm
        ],
        out_specs=hbm,
        scratch_shapes=[
            pltpu.VMEM((TOK, 128), BF),
            pltpu.VMEM((NX, 2 * NB, 16, TOK), BF),
            pltpu.VMEM((NX, 2, 2, TOK, 128), BF),
            pltpu.VMEM((NY, 2 * HALF, 128), F32),
            pltpu.VMEM((HOPS, SUB, 128), BF),
            pltpu.VMEM((HOPS, SUB, 128), BF),
            pltpu.VMEM((NE, 2, 16, 128), BF),
            pltpu.VMEM((2 * NE + 1, 16, 128), BF),
            pltpu.VMEM((SLOTS, 16, 128), BF),
            pltpu.VMEM((NZ, 2, 32, BS), BF),
            pltpu.VMEM((2, BS, BS), BF),
            pltpu.VMEM((BS, BS), F32),
            pltpu.VMEM((BS, BS), F32),
            pltpu.VMEM((4, 128, BS), BF),
            pltpu.VMEM((2, 8, 128), jnp.int32),
            pltpu.SMEM((2, 8, 128), jnp.int32),
            dma((2, 3)), dma((2, 3)), dma(()), dma((2,)), dma((2,)), dma((2,)),
            dma(()), dma((HOPS,)), dma(()), dma(()),
            dma(()), dma(()), dma(()), dma(()), dma((2,)), dma((2,)), dma(()), dma(()), dma(()), dma(()),
            dma((5,)), dma(()), pltpu.SemaphoreType.REGULAR,
        ],
        compiler_params=pltpu.CompilerParams(
            collective_id=0, has_side_effects=True, vmem_limit_bytes=60 * 1024 * 1024
        ),
    )(owner.reshape(-1), col_index, acts, grads_out.T.reshape(NB, 2, 16, TOK), stats.reshape(BS, BS))


def solution(mesh):
    return jax.shard_map(
        shards,
        mesh=mesh,
        in_specs=(P("own", "dp"), P("own", "dp"), P("own", "dp", None, None, None), P(), P()),
        out_specs=P("own", "dp", None, None, None),
        check_vma=False,
    )
```

```python
import jax
import jax.numpy as jnp
from jax import lax
from jax.experimental import pallas as pl
from jax.experimental.pallas import tpu as pltpu
from jax.sharding import PartitionSpec as P

STAT_DECAY = 0.9
EPSILON = 1e-06
MESH = pl.DeviceIdType.MESH
BF = jnp.bfloat16
F32 = jnp.float32
NX, NY, NZ = 4, 8, 8
NE = 2 * NZ
BS = 512
TOK = 128
HALF = 240
SUB = 80
HOPS = 42
NB = 30
SLOTS = 64
ORDER = sorted(
    ((i, k, s) for i in range(NY) for k in range(NX) for s in range(2)),
    key=lambda t: -min(t[0], NY - t[0]) - min(t[1], NX - t[1]),
)
NN = (((1,), (0,)), ((), ()))
NT = (((1,), (1,)), ((), ()))
TN = (((0,), (0,)), ((), ()))


def dot(a, b, dims=NN):
    return lax.dot_general(a, b, dims, preferred_element_type=F32)


def wait(ref, sem):
    pltpu.make_async_copy(ref, ref, sem).wait()


def kernel(
    owner, col_index, acts, grads, stats, out,
    ax, bt, am, part, snd, rcv, summed, tiles, outgoing, h4, rt, stat, work, res, slots, table,
    b_send, b_recv, a_send, a_recv, f_send, f_recv, r_send, r_recv, t_send, t_recv,
    o_send, o_recv, h_send, h_recv, q_send, q_recv, u_send, u_recv, s_sem, g_sem, i_sem, w_sem, know,
):
    own = lax.axis_index("own")
    dp = lax.axis_index("dp")
    y, x = lax.div(own, NX), lax.rem(own, NX)
    z, c = lax.div(dp, 2), lax.rem(dp, 2)
    side = lax.rem(z, 2)
    brow = lax.div(z, 2)
    crow = lax.rem(x + z, NX)
    mine = brow == crow
    spot = 2 * (4 * side + x) + c
    sibling = (own, dp + 1 - 2 * c)
    pair = (own, dp + 2 - 4 * side)

    def ring(step):
        return lax.rem(y + step + NY, NY)

    def remote(src, dst, send_sem, recv_sem, device):
        return pltpu.make_async_remote_copy(
            src_ref=src, dst_ref=dst, send_sem=send_sem, recv_sem=recv_sem,
            device_id=device, device_id_type=MESH,
        )

    pending = []

    acts_copy = pltpu.make_async_copy(acts, ax, i_sem.at[4])
    acts_copy.start()
    grads_copies = [
        pltpu.make_async_copy(
            grads.at[pl.ds(15 * g, 15), h], bt.at[x, pl.ds(15 * (2 * g + h), 15)],
            i_sem.at[2 * g + h],
        )
        for g in range(2)
        for h in range(2)
    ]
    for copy in grads_copies:
        copy.start()
    stat_copy = pltpu.make_async_copy(stats, stat, s_sem)
    stat_copy.start()

    barrier = pltpu.get_barrier_semaphore()

    def say(sem, device):
        pl.semaphore_signal(sem, inc=1, device_id=device, device_id_type=MESH)

    def along_x(step):
        return (y * NX + lax.rem(x + step + NX, NX), dp)

    def along_z(step):
        return (own, 2 * lax.rem(z + step + NZ, NZ) + c)

    for i in (1, 2, 3):
        say(barrier, along_x(i))
    for i in (1, -1, 2, -2):
        say(barrier, (ring(i) * NX + x, dp))
    say(barrier, sibling)
    for i in (1, -1, 2, -2):
        for k in range(NX):
            say(barrier, (along_x(k)[0], along_z(i)[1]))

    acts_copy.wait()
    for copy in grads_copies:
        copy.wait()
    pl.semaphore_wait(barrier, 24)
    for i in (2, -2):
        say(know, along_z(i))

    def pass_on(shard, g, way, kind):
        there = bt.at[shard, pl.ds(30 * g, 30)]
        copy = remote(
            there, there, b_send.at[g, kind], b_recv.at[g, kind], along_x(1 - 2 * way)
        )
        copy.start()
        pending.append(copy.wait_send)

    def arrive(g, kind):
        shard = lax.rem(x + (NX - 1, 1, 2)[kind], NX)
        wait(bt.at[shard, pl.ds(30 * g, 30)], b_recv.at[g, kind])
        return shard

    def inputs_out(i):
        plane = lax.rem(z + i, NZ)
        column = lax.rem(brow - plane + 2 * NX, NX)

        def local():
            pltpu.make_async_copy(ax, am.at[x, side, c], a_recv.at[side]).start()

        def away(plane=plane, column=column):
            remote(
                ax, am.at[x, side, c], a_send, a_recv.at[side], (y * NX + column, 2 * plane + c)
            ).start()

        if i == 0:
            pl.when(mine)(local)
            pl.when(jnp.logical_not(mine))(away)
        else:
            away()

    for i in (2, 6, 1, 7, 0):
        inputs_out(i)
    for g in range(2):
        for way in range(2):
            pass_on(x, (g + way) % 2, way, way)
    pl.semaphore_wait(know, 2)
    for i in (4, 3, 5):
        inputs_out(i)

    summed[...] = jnp.zeros_like(summed)
    tiles[2 * NE] = jnp.zeros((16, 128), BF)

    lane = lax.broadcasted_iota(jnp.int32, (8, 128), 1)
    none = jnp.full((8, 128), NB, jnp.int32)

    def enter(k, taken):
        hit = lane == owner[NB * brow + k]
        free = taken[0] == NB
        return (
            jnp.where(jnp.logical_and(hit, free), col_index[brow, k], taken[0]),
            jnp.where(jnp.logical_and(hit, jnp.logical_not(free)), col_index[brow, k], taken[1]),
        )

    for slot, taken in enumerate(lax.fori_loop(0, NB, enter, (none, none))):
        place = NE * taken + spot
        source = lax.shift_right_logical(place * 2185, 16)
        tile = 2 * source + lax.shift_right_logical(place - NB * source, 4)
        slots[slot] = jnp.where(taken == NB, 2 * NE, tile)
    table_copy = pltpu.make_async_copy(slots, table, g_sem)
    table_copy.start()

    pass_on(arrive(0, 0), 0, 0, 2)
    pass_on(arrive(1, 1), 1, 1, 2)

    @pending.append
    def _():
        @pl.when(mine)
        def _():
            wait(bt.at[0, pl.ds(0, 56)], a_send)

        @pl.when(jnp.logical_not(mine))
        def _():
            wait(am.at[:, :, 0], a_send)

    forwards = []
    for s in range(2):
        wait(am.at[:, s, c], a_recv.at[s])
        forwards.append(
            remote(am.at[:, s, c], am.at[:, s, c], f_send.at[s], f_recv.at[s], sibling)
        )
        forwards[s].start()
        pending.append(forwards[s].wait_send)
    arrive(0, 1)
    arrive(0, 2)
    for copy in forwards:
        copy.wait_recv()

    right = jnp.concatenate(
        [
            jnp.concatenate([am[i, s, k] for s in range(2) for k in range(2)], axis=1)
            for i in range(NX)
        ],
        axis=0,
    )
    def multiply(g):
        for h in range(2):
            rows = pl.ds(15 * (2 * g + h), 15)
            left = jnp.concatenate(
                [bt[i, rows].reshape(HALF, TOK) for i in range(NX)], axis=1
            )
            product = dot(left, right)
            for k in range(4):
                part[4 * h + k, pl.ds(HALF * g, HALF), :] = product[:, 128 * k : 128 * k + 128]

    where = {}
    for stage in range(4):
        for way in range(2):
            for sub in range(6):
                if stage or sub % 2 != way:
                    where[way, stage, sub] = len(where)

    def hop(way, stage, sub):
        sign = 1 - 2 * way
        value = part[ring(sign * (4 - stage)), pl.ds(SUB * sub, SUB), :]
        for last in ((0, 1) if stage == 2 else (2,) if stage == 3 else ()):
            if (way, last, sub) in where:
                last = where[way, last, sub]
                wait(rcv.at[last], r_recv.at[last])
                value = value + rcv[last].astype(F32)
        now = where[way, stage, sub]
        snd[now] = value.astype(BF)
        target = ring(sign * (1 if stage else 2)) * NX + x
        remote(snd.at[now], rcv.at[now], r_send, r_recv.at[now], (target, dp)).start()

    def begin(g):
        multiply(g)
        for i in range(3 * g, 3 * g + 3):
            hop(1 - i % 2, 0, i)
        for i in range(3 * g, 3 * g + 3):
            hop(1, 1, i)
            hop(0, 1, i)

    begin(0)
    arrive(1, 0)
    arrive(1, 2)
    begin(1)
    for stage in (2, 3):
        for i in range(6):
            hop(1, stage, i)
            hop(0, stage, i)
    pending.append(lambda: wait(snd, r_send))
    for sub in range(6):
        value = part[y, pl.ds(SUB * sub, SUB), :]
        for way in range(2):
            last = where[way, 3, sub]
            wait(rcv.at[last], r_recv.at[last])
            value = value + rcv[last].astype(F32)
        value = value.astype(BF).reshape(5, 16, 128)
        for i in range(5):
            k = 5 * sub + i
            summed[lax.rem(NB * dp + k, NE), k // NE] = value[i]

    for i in (2, 1, 3, 0):
        for s in range(2):
            for k in range(2):
                column = lax.rem(x + i, NX)
                target = 2 * (2 * crow + s) + k
                tile = 2 * (4 * s + column) + k
                here = target == dp if i == 0 else False

                def local(tile=tile):
                    pltpu.make_async_copy(
                        summed.at[tile], tiles.at[pl.ds(2 * dp, 2)], t_recv
                    ).start()

                def away(tile=tile, column=column, target=target):
                    remote(
                        summed.at[tile], tiles.at[pl.ds(2 * dp, 2)], t_send, t_recv,
                        (y * NX + column, target),
                    ).start()

                if i == 0:
                    pl.when(here)(local)
                    pl.when(jnp.logical_not(here))(away)
                else:
                    away()

    @pending.append
    def _():
        @pl.when(mine)
        def _():
            wait(summed.at[pl.ds(0, NE - 1)], t_send)

        @pl.when(jnp.logical_not(mine))
        def _():
            wait(summed, t_send)

    wait(tiles.at[pl.ds(0, 2 * NE)], t_recv)

    lanes = pl.ds(pl.multiple_of(128 * lax.rem(y, 4), 128), 128)
    rows = pl.ds(pl.multiple_of(16 * lax.div(y, 4), 16), 16)

    here = h4.at[side, x, c, rows, lanes]
    table_copy.wait()
    for batch in range(0, SLOTS, 16):
        places = list(enumerate(ORDER))[batch : batch + 16]
        held = [ring(i) * NX + lax.rem(x + k, NX) for _, (i, k, s) in places]
        for (count, (i, k, s)), owner_id in zip(places, held):
            outgoing[count] = tiles[table[s, 0, owner_id]]
        for (count, (i, k, s)), owner_id in zip(places, held):
            target = 2 * (2 * brow + s) + c

            def local(count=count):
                pltpu.make_async_copy(outgoing.at[count], here, o_recv.at[side]).start()

            def away(count=count, owner_id=owner_id, target=target):
                remote(
                    outgoing.at[count], here, o_send, o_recv.at[side], (owner_id, target)
                ).start()

            if i == 0 and k == 0:
                pl.when(side == s)(local)
                pl.when(side != s)(away)
            else:
                away()

    pending.append(lambda: wait(outgoing.at[pl.ds(0, SLOTS - 1)], o_send))
    swaps = []
    for s in range(2):
        wait(h4.at[s, :, c], o_recv.at[s])
        swaps.append(remote(h4.at[s, :, c], h4.at[s, :, c], h_send.at[s], h_recv.at[s], sibling))
        swaps[s].start()
        pending.append(swaps[s].wait_send)
    stat_copy.wait()
    for copy in swaps:
        copy.wait_recv()

    block = h4[...].reshape(BS, BS)

    @pl.when(c == 0)
    def _():
        work[...] = dot(block, block, TN)

    @pl.when(c != 0)
    def _():
        work[...] = dot(block, block, NT)

    factor = STAT_DECAY * stat[...] + (1.0 - STAT_DECAY) * work[...]
    eye = lax.broadcasted_iota(jnp.int32, (BS, BS), 0) == lax.broadcasted_iota(
        jnp.int32, (BS, BS), 1
    )
    scale = jnp.sum(jnp.where(eye, factor, 0.0)) / BS + EPSILON
    first = (jnp.where(eye, 5.0, 0.0) - factor / scale) / 4.0
    near = first.astype(BF)
    square = dot(near, near)
    rest = (5.0 * near.astype(F32) - 4.0 * square).astype(BF)
    square = square.astype(BF)
    fourth = dot(square, square).astype(BF)
    roots = []
    for k in range(2):
        rows = slice(BS // 2 * k, BS // 2 * k + BS // 2)
        moved = dot(fourth[rows], rest)
        there = rt.at[c, pl.ds(BS // 2 * k, BS // 2)]
        rt[c, pl.ds(BS // 2 * k, BS // 2), :] = ((5.0 * first[rows] - moved) / 4.0).astype(BF)
        roots.append(remote(there, there, q_send.at[k], q_recv.at[k], sibling))
        roots[k].start()
        pending.append(roots[k].wait_send)
    wide = block.astype(F32)
    grad_scale = jnp.sqrt(jnp.sum(wide * wide) / (BS * BS) + EPSILON)
    for copy in roots:
        copy.wait_recv()

    carried = dot(rt[0], block, NT).astype(BF)
    whole = dot(carried, rt[1])
    prec_scale = jnp.sqrt(jnp.sum(whole * whole) / (BS * BS) + EPSILON)
    wide_rows = BS // 4
    work[...] = whole
    for k in range(2):
        quarter = pl.ds(pl.multiple_of(wide_rows * (2 * k + c), wide_rows), wide_rows)
        res[k] = (work[quarter, :] * (grad_scale / prec_scale)).astype(BF)
    keep = pltpu.make_async_copy(res.at[side], out.at[0, 0, side], w_sem)
    last = remote(res.at[1 - side], out.at[0, 0, side], u_send, u_recv, pair)
    last.start()
    keep.start()
    pending.append(last.wait_send)
    pending.append(keep.wait)
    last.wait_recv()

    for done in pending:
        done()


def shards(acts, grads_out, stats, owner, col_index):
    dma = pltpu.SemaphoreType.DMA
    smem = pl.BlockSpec(memory_space=pltpu.SMEM)
    hbm = pl.BlockSpec(memory_space=pl.ANY)
    return pl.pallas_call(
        kernel,
        out_shape=jax.ShapeDtypeStruct((1, 1, 2, 128, BS), BF),
        in_specs=[
            smem, smem, hbm, hbm, hbm
        ],
        out_specs=hbm,
        scratch_shapes=[
            pltpu.VMEM((TOK, 128), BF),
            pltpu.VMEM((NX, 2 * NB, 16, TOK), BF),
            pltpu.VMEM((NX, 2, 2, TOK, 128), BF),
            pltpu.VMEM((NY, 2 * HALF, 128), F32),
            pltpu.VMEM((HOPS, SUB, 128), BF),
            pltpu.VMEM((HOPS, SUB, 128), BF),
            pltpu.VMEM((NE, 2, 16, 128), BF),
            pltpu.VMEM((2 * NE + 1, 16, 128), BF),
            pltpu.VMEM((SLOTS, 16, 128), BF),
            pltpu.VMEM((2, NX, 2, 32, BS), BF),
            pltpu.VMEM((2, BS, BS), BF),
            pltpu.VMEM((BS, BS), F32),
            pltpu.VMEM((BS, BS), F32),
            pltpu.VMEM((2, 128, BS), BF),
            pltpu.VMEM((2, 8, 128), jnp.int32),
            pltpu.SMEM((2, 8, 128), jnp.int32),
            dma((2, 3)), dma((2, 3)), dma(()), dma((2,)), dma((2,)), dma((2,)),
            dma(()), dma((HOPS,)), dma(()), dma(()),
            dma(()), dma((2,)), dma((2,)), dma((2,)), dma((2,)), dma((2,)), dma(()), dma(()), dma(()), dma(()),
            dma((5,)), dma(()), pltpu.SemaphoreType.REGULAR,
        ],
        compiler_params=pltpu.CompilerParams(
            collective_id=0, has_side_effects=True, vmem_limit_bytes=60 * 1024 * 1024
        ),
    )(owner.reshape(-1), col_index, acts, grads_out.T.reshape(NB, 2, 16, TOK), stats.reshape(BS, BS))


def solution(mesh):
    return jax.shard_map(
        shards,
        mesh=mesh,
        in_specs=(P("own", "dp"), P("own", "dp"), P("own", "dp", None, None, None), P(), P()),
        out_specs=P("own", "dp", None, None, None),
        check_vma=False,
    )
```

```python
import jax
import jax.numpy as jnp
from jax import lax
from jax.experimental import pallas as pl
from jax.experimental.pallas import tpu as pltpu
from jax.sharding import PartitionSpec as P

STAT_DECAY = 0.9
EPSILON = 1e-06
MESH = pl.DeviceIdType.MESH
BF = jnp.bfloat16
F32 = jnp.float32
NX, NY, NZ = 4, 8, 8
NE = 2 * NZ
BS = 512
TOK = 128
HALF = 240
SUB = 80
HOPS = 42
NB = 30
SLOTS = 64
ORDER = sorted(
    ((i, k, s) for i in range(NY) for k in range(NX) for s in range(2)),
    key=lambda t: -min(t[0], NY - t[0]) - min(t[1], NX - t[1]),
)
NN = (((1,), (0,)), ((), ()))
NT = (((1,), (1,)), ((), ()))
TN = (((0,), (0,)), ((), ()))


def dot(a, b, dims=NN):
    return lax.dot_general(a, b, dims, preferred_element_type=F32)


def wait(ref, sem):
    pltpu.make_async_copy(ref, ref, sem).wait()


def kernel(
    owner, col_index, acts, grads, stats, out, scales,
    ax, bt, am, part, snd, rcv, summed, tiles, outgoing, h4, rt, stat, work, res, graft, slots, table,
    b_send, b_recv, a_send, a_recv, f_send, f_recv, r_send, r_recv, t_send, t_recv,
    o_send, o_recv, h_send, h_recv, q_send, q_recv, u_send, u_recv, s_sem, g_sem, i_sem, w_sem, know,
):
    own = lax.axis_index("own")
    dp = lax.axis_index("dp")
    y, x = lax.div(own, NX), lax.rem(own, NX)
    z, c = lax.div(dp, 2), lax.rem(dp, 2)
    side = lax.rem(z, 2)
    brow = lax.div(z, 2)
    crow = lax.rem(x + z, NX)
    mine = brow == crow
    spot = 2 * (4 * side + x) + c
    sibling = (own, dp + 1 - 2 * c)
    pair = (own, dp + 2 - 4 * side)

    def ring(step):
        return lax.rem(y + step + NY, NY)

    def remote(src, dst, send_sem, recv_sem, device):
        return pltpu.make_async_remote_copy(
            src_ref=src, dst_ref=dst, send_sem=send_sem, recv_sem=recv_sem,
            device_id=device, device_id_type=MESH,
        )

    pending = []

    acts_copy = pltpu.make_async_copy(acts, ax, i_sem.at[4])
    acts_copy.start()
    grads_copies = [
        pltpu.make_async_copy(
            grads.at[pl.ds(15 * g, 15), h], bt.at[x, pl.ds(15 * (2 * g + h), 15)],
            i_sem.at[2 * g + h],
        )
        for g in range(2)
        for h in range(2)
    ]
    for copy in grads_copies:
        copy.start()
    stat_copy = pltpu.make_async_copy(stats, stat, s_sem)
    stat_copy.start()

    barrier = pltpu.get_barrier_semaphore()

    def say(sem, device):
        pl.semaphore_signal(sem, inc=1, device_id=device, device_id_type=MESH)

    def along_x(step):
        return (y * NX + lax.rem(x + step + NX, NX), dp)

    def along_z(step):
        return (own, 2 * lax.rem(z + step + NZ, NZ) + c)

    for i in (1, 2, 3):
        say(barrier, along_x(i))
    for i in (1, -1, 2, -2):
        say(barrier, (ring(i) * NX + x, dp))
    say(barrier, sibling)
    for i in (1, -1, 2, -2):
        for k in range(NX):
            say(barrier, (along_x(k)[0], along_z(i)[1]))

    acts_copy.wait()
    for copy in grads_copies:
        copy.wait()
    pl.semaphore_wait(barrier, 24)
    for i in (2, -2):
        say(know, along_z(i))

    def pass_on(shard, g, way, kind):
        there = bt.at[shard, pl.ds(30 * g, 30)]
        copy = remote(
            there, there, b_send.at[g, kind], b_recv.at[g, kind], along_x(1 - 2 * way)
        )
        copy.start()
        pending.append(copy.wait_send)

    def arrive(g, kind):
        shard = lax.rem(x + (NX - 1, 1, 2)[kind], NX)
        wait(bt.at[shard, pl.ds(30 * g, 30)], b_recv.at[g, kind])
        return shard

    def inputs_out(i):
        plane = lax.rem(z + i, NZ)
        column = lax.rem(brow - plane + 2 * NX, NX)

        def local():
            pltpu.make_async_copy(ax, am.at[x, side, c], a_recv.at[side]).start()

        def away(plane=plane, column=column):
            remote(
                ax, am.at[x, side, c], a_send, a_recv.at[side], (y * NX + column, 2 * plane + c)
            ).start()

        if i == 0:
            pl.when(mine)(local)
            pl.when(jnp.logical_not(mine))(away)
        else:
            away()

    for i in (2, 6, 1, 7, 0):
        inputs_out(i)
    for g in range(2):
        for way in range(2):
            pass_on(x, (g + way) % 2, way, way)
    pl.semaphore_wait(know, 2)
    for i in (4, 3, 5):
        inputs_out(i)

    summed[...] = jnp.zeros_like(summed)
    tiles[2 * NE] = jnp.zeros((16, 128), BF)

    lane = lax.broadcasted_iota(jnp.int32, (8, 128), 1)
    none = jnp.full((8, 128), NB, jnp.int32)

    def enter(k, taken):
        hit = lane == owner[NB * brow + k]
        free = taken[0] == NB
        return (
            jnp.where(jnp.logical_and(hit, free), col_index[brow, k], taken[0]),
            jnp.where(jnp.logical_and(hit, jnp.logical_not(free)), col_index[brow, k], taken[1]),
        )

    for slot, taken in enumerate(lax.fori_loop(0, NB, enter, (none, none))):
        place = NE * taken + spot
        source = lax.shift_right_logical(place * 2185, 16)
        tile = 2 * source + lax.shift_right_logical(place - NB * source, 4)
        slots[slot] = jnp.where(taken == NB, 2 * NE, tile)
    table_copy = pltpu.make_async_copy(slots, table, g_sem)
    table_copy.start()

    pass_on(arrive(0, 0), 0, 0, 2)
    pass_on(arrive(1, 1), 1, 1, 2)

    @pending.append
    def _():
        @pl.when(mine)
        def _():
            wait(bt.at[0, pl.ds(0, 56)], a_send)

        @pl.when(jnp.logical_not(mine))
        def _():
            wait(am.at[:, :, 0], a_send)

    forwards = []
    for s in range(2):
        wait(am.at[:, s, c], a_recv.at[s])
        forwards.append(
            remote(am.at[:, s, c], am.at[:, s, c], f_send.at[s], f_recv.at[s], sibling)
        )
        forwards[s].start()
        pending.append(forwards[s].wait_send)
    arrive(0, 1)
    arrive(0, 2)
    for copy in forwards:
        copy.wait_recv()

    right = jnp.concatenate(
        [
            jnp.concatenate([am[i, s, k] for s in range(2) for k in range(2)], axis=1)
            for i in range(NX)
        ],
        axis=0,
    )

    def multiply(g):
        left = jnp.concatenate(
            [bt[i, pl.ds(30 * g, 30)].reshape(2 * HALF, TOK) for i in range(NX)], axis=1
        )
        product = dot(left, right)
        for h in range(2):
            for k in range(4):
                part[4 * h + k, pl.ds(HALF * g, HALF), :] = product[
                    HALF * h : HALF * h + HALF, 128 * k : 128 * k + 128
                ]

    where = {}
    for stage in range(4):
        for way in range(2):
            for sub in range(6):
                if stage or sub % 2 != way:
                    where[way, stage, sub] = len(where)

    def hop(way, stage, sub):
        sign = 1 - 2 * way
        value = part[ring(sign * (4 - stage)), pl.ds(SUB * sub, SUB), :]
        for last in ((0, 1) if stage == 2 else (2,) if stage == 3 else ()):
            if (way, last, sub) in where:
                last = where[way, last, sub]
                wait(rcv.at[last], r_recv.at[last])
                value = value + rcv[last].astype(F32)
        now = where[way, stage, sub]
        snd[now] = value.astype(BF)
        target = ring(sign * (1 if stage else 2)) * NX + x
        remote(snd.at[now], rcv.at[now], r_send, r_recv.at[now], (target, dp)).start()

    def begin(g):
        multiply(g)
        for i in range(3 * g, 3 * g + 3):
            hop(1 - i % 2, 0, i)
        for i in range(3 * g, 3 * g + 3):
            hop(1, 1, i)
            hop(0, 1, i)

    begin(0)
    arrive(1, 0)
    arrive(1, 2)
    begin(1)
    for stage in (2, 3):
        for i in range(6):
            hop(1, stage, i)
            hop(0, stage, i)
    pending.append(lambda: wait(snd, r_send))
    for sub in range(6):
        value = part[y, pl.ds(SUB * sub, SUB), :]
        for way in range(2):
            last = where[way, 3, sub]
            wait(rcv.at[last], r_recv.at[last])
            value = value + rcv[last].astype(F32)
        value = value.astype(BF).reshape(5, 16, 128)
        for i in range(5):
            k = 5 * sub + i
            summed[lax.rem(NB * dp + k, NE), k // NE] = value[i]

    for i in (2, 1, 3, 0):
        for s in range(2):
            for k in range(2):
                column = lax.rem(x + i, NX)
                target = 2 * (2 * crow + s) + k
                tile = 2 * (4 * s + column) + k
                here = target == dp if i == 0 else False

                def local(tile=tile):
                    pltpu.make_async_copy(
                        summed.at[tile], tiles.at[pl.ds(2 * dp, 2)], t_recv
                    ).start()

                def away(tile=tile, column=column, target=target):
                    remote(
                        summed.at[tile], tiles.at[pl.ds(2 * dp, 2)], t_send, t_recv,
                        (y * NX + column, target),
                    ).start()

                if i == 0:
                    pl.when(here)(local)
                    pl.when(jnp.logical_not(here))(away)
                else:
                    away()

    @pending.append
    def _():
        @pl.when(mine)
        def _():
            wait(summed.at[pl.ds(0, NE - 1)], t_send)

        @pl.when(jnp.logical_not(mine))
        def _():
            wait(summed, t_send)

    wait(tiles.at[pl.ds(0, 2 * NE)], t_recv)

    lanes = pl.ds(pl.multiple_of(128 * lax.rem(y, 4), 128), 128)
    rows = pl.ds(pl.multiple_of(16 * lax.div(y, 4), 16), 16)

    here = h4.at[side, x, c, rows, lanes]
    table_copy.wait()
    for batch in range(0, SLOTS, 16):
        places = list(enumerate(ORDER))[batch : batch + 16]
        held = [ring(i) * NX + lax.rem(x + k, NX) for _, (i, k, s) in places]
        for (count, (i, k, s)), owner_id in zip(places, held):
            outgoing[count] = tiles[table[s, 0, owner_id]]
        for (count, (i, k, s)), owner_id in zip(places, held):
            target = 2 * (2 * brow + s) + c

            def local(count=count):
                pltpu.make_async_copy(outgoing.at[count], here, o_recv.at[side]).start()

            def away(count=count, owner_id=owner_id, target=target):
                remote(
                    outgoing.at[count], here, o_send, o_recv.at[side], (owner_id, target)
                ).start()

            if i == 0 and k == 0:
                pl.when(side == s)(local)
                pl.when(side != s)(away)
            else:
                away()

    pending.append(lambda: wait(outgoing.at[pl.ds(0, SLOTS - 1)], o_send))
    swaps = []
    for s in range(2):
        wait(h4.at[s, :, c], o_recv.at[s])
        swaps.append(remote(h4.at[s, :, c], h4.at[s, :, c], h_send.at[s], h_recv.at[s], sibling))
        swaps[s].start()
        pending.append(swaps[s].wait_send)
    stat_copy.wait()
    for copy in swaps:
        copy.wait_recv()

    block = h4[...].reshape(BS, BS)

    @pl.when(c == 0)
    def _():
        work[...] = dot(block, block, TN)

    @pl.when(c != 0)
    def _():
        work[...] = dot(block, block, NT)

    factor = STAT_DECAY * stat[...] + (1.0 - STAT_DECAY) * work[...]
    eye = lax.broadcasted_iota(jnp.int32, (BS, BS), 0) == lax.broadcasted_iota(
        jnp.int32, (BS, BS), 1
    )
    scale = jnp.sum(jnp.where(eye, factor, 0.0)) / BS + EPSILON
    first = (jnp.where(eye, 5.0, 0.0) - factor / scale) / 4.0
    near = first.astype(BF)
    square = dot(near, near)
    rest = (5.0 * near.astype(F32) - 4.0 * square).astype(BF)
    square = square.astype(BF)
    fourth = dot(square, square).astype(BF)
    roots = []
    for k in range(2):
        rows = slice(BS // 2 * k, BS // 2 * k + BS // 2)
        moved = dot(fourth[rows], rest)
        there = rt.at[c, pl.ds(BS // 2 * k, BS // 2)]
        rt[c, pl.ds(BS // 2 * k, BS // 2), :] = ((5.0 * first[rows] - moved) / 4.0).astype(BF)
        roots.append(remote(there, there, q_send.at[k], q_recv.at[k], sibling))
        roots[k].start()
        pending.append(roots[k].wait_send)
    wide = block.astype(F32)
    grad_scale = jnp.sqrt(jnp.sum(wide * wide) / (BS * BS) + EPSILON)
    for copy in roots:
        copy.wait_recv()

    quarter = pl.ds(pl.multiple_of(128 * (2 * (1 - side) + c), 128), 128)
    carried = dot(rt[0, quarter, :], block, NT).astype(BF)
    res[1] = dot(carried, rt[1]).astype(BF)
    last = remote(res.at[1], out.at[0, 0, side], u_send.at[0], u_recv.at[0], pair)
    last.start()
    pending.append(last.wait_send)
    carried = dot(rt[0], block, NT).astype(BF)
    whole = dot(carried, rt[1])
    work[...] = whole
    quarter = pl.ds(pl.multiple_of(128 * (2 * side + c), 128), 128)
    res[0] = work[quarter, :].astype(BF)
    keep = pltpu.make_async_copy(res.at[0], out.at[0, 0, side], w_sem.at[0])
    keep.start()
    pending.append(keep.wait)
    prec_scale = jnp.sqrt(jnp.sum(whole * whole) / (BS * BS) + EPSILON)
    graft[...] = jnp.full(graft.shape, grad_scale / prec_scale, F32)
    scale_out = remote(graft, scales.at[side], u_send.at[1], u_recv.at[1], pair)
    scale_out.start()
    pending.append(scale_out.wait_send)
    keep_scale = pltpu.make_async_copy(graft, scales.at[side], w_sem.at[1])
    keep_scale.start()
    pending.append(keep_scale.wait)
    last.wait_recv()
    scale_out.wait_recv()

    for done in pending:
        done()


def shards(acts, grads_out, stats, owner, col_index):
    dma = pltpu.SemaphoreType.DMA
    smem = pl.BlockSpec(memory_space=pltpu.SMEM)
    hbm = pl.BlockSpec(memory_space=pl.ANY)
    raw, scales = pl.pallas_call(
        kernel,
        out_shape=(
            jax.ShapeDtypeStruct((1, 1, 2, 128, BS), BF),
            jax.ShapeDtypeStruct((2, 8, BS), F32),
        ),
        in_specs=[
            smem, smem, hbm, hbm, hbm
        ],
        out_specs=(hbm, hbm),
        scratch_shapes=[
            pltpu.VMEM((TOK, 128), BF),
            pltpu.VMEM((NX, 2 * NB, 16, TOK), BF),
            pltpu.VMEM((NX, 2, 2, TOK, 128), BF),
            pltpu.VMEM((NY, 2 * HALF, 128), F32),
            pltpu.VMEM((HOPS, SUB, 128), BF),
            pltpu.VMEM((HOPS, SUB, 128), BF),
            pltpu.VMEM((NE, 2, 16, 128), BF),
            pltpu.VMEM((2 * NE + 1, 16, 128), BF),
            pltpu.VMEM((SLOTS, 16, 128), BF),
            pltpu.VMEM((2, NX, 2, 32, BS), BF),
            pltpu.VMEM((2, BS, BS), BF),
            pltpu.VMEM((BS, BS), F32),
            pltpu.VMEM((BS, BS), F32),
            pltpu.VMEM((2, 128, BS), BF),
            pltpu.VMEM((8, BS), F32),
            pltpu.VMEM((2, 8, 128), jnp.int32),
            pltpu.SMEM((2, 8, 128), jnp.int32),
            dma((2, 3)), dma((2, 3)), dma(()), dma((2,)), dma((2,)), dma((2,)),
            dma(()), dma((HOPS,)), dma(()), dma(()),
            dma(()), dma((2,)), dma((2,)), dma((2,)), dma((2,)), dma((2,)), dma((2,)), dma((2,)), dma(()), dma(()),
            dma((5,)), dma((2,)), pltpu.SemaphoreType.REGULAR,
        ],
        compiler_params=pltpu.CompilerParams(
            collective_id=0, has_side_effects=True, vmem_limit_bytes=60 * 1024 * 1024
        ),
    )(owner.reshape(-1), col_index, acts, grads_out.T.reshape(NB, 2, 16, TOK), stats.reshape(BS, BS))
    scaled = raw.reshape(2, 16, 8, BS).astype(F32) * scales[:, None]
    return scaled.astype(BF).reshape(raw.shape)


def solution(mesh):
    return jax.shard_map(
        shards,
        mesh=mesh,
        in_specs=(P("own", "dp"), P("own", "dp"), P("own", "dp", None, None, None), P(), P()),
        out_specs=P("own", "dp", None, None, None),
        check_vma=False,
    )
```

```python
import jax
import jax.numpy as jnp
from jax import lax
from jax.experimental import pallas as pl
from jax.experimental.pallas import tpu as pltpu
from jax.sharding import PartitionSpec as P

STAT_DECAY = 0.9
EPSILON = 1e-06
MESH = pl.DeviceIdType.MESH
BF = jnp.bfloat16
F32 = jnp.float32
NX, NY, NZ = 4, 8, 8
NE = 2 * NZ
BS = 512
TOK = 128
HALF = 240
SUB = 80
HOPS = 42
NB = 30
SLOTS = 64
ORDER = sorted(
    ((i, k, s) for i in range(NY) for k in range(NX) for s in range(2)),
    key=lambda t: -min(t[0], NY - t[0]) - min(t[1], NX - t[1]) - t[2],
)
NN = (((1,), (0,)), ((), ()))
NT = (((1,), (1,)), ((), ()))
TN = (((0,), (0,)), ((), ()))


def dot(a, b, dims=NN):
    return lax.dot_general(a, b, dims, preferred_element_type=F32)


def wait(ref, sem):
    pltpu.make_async_copy(ref, ref, sem).wait()


def kernel(
    owner, col_index, acts, grads, stats, out, scales,
    ax, bt, am, part, snd, rcv, summed, tiles, outgoing, h4, rt, stat, work, res, graft, slots, table,
    b_send, b_recv, a_send, a_recv, f_send, f_recv, r_send, r_recv, t_send, t_recv,
    o_send, o_recv, h_send, h_recv, q_send, q_recv, u_send, u_recv, s_sem, g_sem, i_sem, w_sem, know,
):
    own = lax.axis_index("own")
    dp = lax.axis_index("dp")
    y, x = lax.div(own, NX), lax.rem(own, NX)
    z, c = lax.div(dp, 2), lax.rem(dp, 2)
    side = lax.rem(z, 2)
    brow = lax.div(z, 2)
    crow = lax.rem(x + z, NX)
    mine = brow == crow
    spot = 2 * (4 * side + x) + c
    sibling = (own, dp + 1 - 2 * c)
    pair = (own, dp + 2 - 4 * side)

    def ring(step):
        return lax.rem(y + step + NY, NY)

    def remote(src, dst, send_sem, recv_sem, device):
        return pltpu.make_async_remote_copy(
            src_ref=src, dst_ref=dst, send_sem=send_sem, recv_sem=recv_sem,
            device_id=device, device_id_type=MESH,
        )

    pending = []

    acts_copy = pltpu.make_async_copy(acts, ax, i_sem.at[4])
    acts_copy.start()
    grads_copies = [
        pltpu.make_async_copy(
            grads.at[pl.ds(15 * g, 15), h], bt.at[x, pl.ds(15 * (2 * g + h), 15)],
            i_sem.at[2 * g + h],
        )
        for g in range(2)
        for h in range(2)
    ]
    for copy in grads_copies:
        copy.start()
    stat_copy = pltpu.make_async_copy(stats, stat, s_sem)
    stat_copy.start()

    barrier = pltpu.get_barrier_semaphore()

    def say(sem, device):
        pl.semaphore_signal(sem, inc=1, device_id=device, device_id_type=MESH)

    def along_x(step):
        return (y * NX + lax.rem(x + step + NX, NX), dp)

    def along_z(step):
        return (own, 2 * lax.rem(z + step + NZ, NZ) + c)

    for i in (1, 2, 3):
        say(barrier, along_x(i))
    for i in (1, -1, 2, -2):
        say(barrier, (ring(i) * NX + x, dp))
    say(barrier, sibling)
    for i in (1, -1, 2, -2):
        for k in range(NX):
            say(barrier, (along_x(k)[0], along_z(i)[1]))

    acts_copy.wait()
    for copy in grads_copies:
        copy.wait()
    pl.semaphore_wait(barrier, 24)
    for i in (2, -2):
        say(know, along_z(i))

    def pass_on(shard, g, way, kind):
        there = bt.at[shard, pl.ds(30 * g, 30)]
        copy = remote(
            there, there, b_send.at[g, kind], b_recv.at[g, kind], along_x(1 - 2 * way)
        )
        copy.start()
        pending.append(copy.wait_send)

    def arrive(g, kind):
        shard = lax.rem(x + (NX - 1, 1, 2)[kind], NX)
        wait(bt.at[shard, pl.ds(30 * g, 30)], b_recv.at[g, kind])
        return shard

    def inputs_out(i):
        plane = lax.rem(z + i, NZ)
        column = lax.rem(brow - plane + 2 * NX, NX)

        def local():
            pltpu.make_async_copy(ax, am.at[x, side, c], a_recv.at[side]).start()

        def away(plane=plane, column=column):
            remote(
                ax, am.at[x, side, c], a_send, a_recv.at[side], (y * NX + column, 2 * plane + c)
            ).start()

        if i == 0:
            pl.when(mine)(local)
            pl.when(jnp.logical_not(mine))(away)
        else:
            away()

    for i in (2, 6, 1, 7, 0):
        inputs_out(i)
    for g in range(2):
        for way in range(2):
            pass_on(x, (g + way) % 2, way, way)
    pl.semaphore_wait(know, 2)
    for i in (4, 3, 5):
        inputs_out(i)

    summed[...] = jnp.zeros_like(summed)
    tiles[2 * NE] = jnp.zeros((16, 128), BF)

    lane = lax.broadcasted_iota(jnp.int32, (8, 128), 1)
    none = jnp.full((8, 128), NB, jnp.int32)

    def enter(k, taken):
        hit = lane == owner[NB * brow + k]
        free = taken[0] == NB
        return (
            jnp.where(jnp.logical_and(hit, free), col_index[brow, k], taken[0]),
            jnp.where(jnp.logical_and(hit, jnp.logical_not(free)), col_index[brow, k], taken[1]),
        )

    for slot, taken in enumerate(lax.fori_loop(0, NB, enter, (none, none))):
        place = NE * taken + spot
        source = lax.shift_right_logical(place * 2185, 16)
        tile = 2 * source + lax.shift_right_logical(place - NB * source, 4)
        slots[slot] = jnp.where(taken == NB, 2 * NE, tile)
    table_copy = pltpu.make_async_copy(slots, table, g_sem)
    table_copy.start()

    pass_on(arrive(0, 0), 0, 0, 2)
    pass_on(arrive(1, 1), 1, 1, 2)

    @pending.append
    def _():
        @pl.when(mine)
        def _():
            wait(bt.at[0, pl.ds(0, 56)], a_send)

        @pl.when(jnp.logical_not(mine))
        def _():
            wait(am.at[:, :, 0], a_send)

    forwards = []
    for s in range(2):
        wait(am.at[:, s, c], a_recv.at[s])
        forwards.append(
            remote(am.at[:, s, c], am.at[:, s, c], f_send.at[s], f_recv.at[s], sibling)
        )
        forwards[s].start()
        pending.append(forwards[s].wait_send)
    arrive(0, 1)
    arrive(0, 2)
    for copy in forwards:
        copy.wait_recv()

    right = jnp.concatenate(
        [
            jnp.concatenate([am[i, s, k] for s in range(2) for k in range(2)], axis=1)
            for i in range(NX)
        ],
        axis=0,
    )

    def multiply(g):
        left = jnp.concatenate(
            [bt[i, pl.ds(30 * g, 30)].reshape(2 * HALF, TOK) for i in range(NX)], axis=1
        )
        product = dot(left, right)
        for h in range(2):
            for k in range(4):
                part[4 * h + k, pl.ds(HALF * g, HALF), :] = product[
                    HALF * h : HALF * h + HALF, 128 * k : 128 * k + 128
                ]

    where = {}
    for stage in range(4):
        for way in range(2):
            for sub in range(6):
                if stage or sub % 2 != way:
                    where[way, stage, sub] = len(where)

    def hop(way, stage, sub):
        sign = 1 - 2 * way
        value = part[ring(sign * (4 - stage)), pl.ds(SUB * sub, SUB), :]
        for last in ((0, 1) if stage == 2 else (2,) if stage == 3 else ()):
            if (way, last, sub) in where:
                last = where[way, last, sub]
                wait(rcv.at[last], r_recv.at[last])
                value = value + rcv[last].astype(F32)
        now = where[way, stage, sub]
        snd[now] = value.astype(BF)
        target = ring(sign * (1 if stage else 2)) * NX + x
        remote(snd.at[now], rcv.at[now], r_send, r_recv.at[now], (target, dp)).start()

    def begin(g):
        multiply(g)
        for i in range(3 * g, 3 * g + 3):
            hop(1 - i % 2, 0, i)
        for i in range(3 * g, 3 * g + 3):
            hop(1, 1, i)
            hop(0, 1, i)

    begin(0)
    arrive(1, 0)
    arrive(1, 2)
    begin(1)
    for stage in (2, 3):
        for i in range(6):
            hop(1, stage, i)
            hop(0, stage, i)
    pending.append(lambda: wait(snd, r_send))
    for sub in range(6):
        value = part[y, pl.ds(SUB * sub, SUB), :]
        for way in range(2):
            last = where[way, 3, sub]
            wait(rcv.at[last], r_recv.at[last])
            value = value + rcv[last].astype(F32)
        value = value.astype(BF).reshape(5, 16, 128)
        for i in range(5):
            k = 5 * sub + i
            summed[lax.rem(NB * dp + k, NE), k // NE] = value[i]

    for i in (2, 1, 3, 0):
        for s in range(2):
            for k in range(2):
                column = lax.rem(x + i, NX)
                target = 2 * (2 * crow + s) + k
                tile = 2 * (4 * s + column) + k
                here = target == dp if i == 0 else False

                def local(tile=tile):
                    pltpu.make_async_copy(
                        summed.at[tile], tiles.at[pl.ds(2 * dp, 2)], t_recv
                    ).start()

                def away(tile=tile, column=column, target=target):
                    remote(
                        summed.at[tile], tiles.at[pl.ds(2 * dp, 2)], t_send, t_recv,
                        (y * NX + column, target),
                    ).start()

                if i == 0:
                    pl.when(here)(local)
                    pl.when(jnp.logical_not(here))(away)
                else:
                    away()

    @pending.append
    def _():
        @pl.when(mine)
        def _():
            wait(summed.at[pl.ds(0, NE - 1)], t_send)

        @pl.when(jnp.logical_not(mine))
        def _():
            wait(summed, t_send)

    wait(tiles.at[pl.ds(0, 2 * NE)], t_recv)

    lanes = pl.ds(pl.multiple_of(128 * lax.rem(y, 4), 128), 128)
    rows = pl.ds(pl.multiple_of(16 * lax.div(y, 4), 16), 16)

    here = h4.at[side, x, c, rows, lanes]
    table_copy.wait()
    for batch in range(0, SLOTS, 16):
        places = list(enumerate(ORDER))[batch : batch + 16]
        held = [ring(i) * NX + lax.rem(x + k, NX) for _, (i, k, s) in places]
        for (count, (i, k, s)), owner_id in zip(places, held):
            outgoing[count] = tiles[table[1 - side if s else side, 0, owner_id]]
        for (count, (i, k, s)), owner_id in zip(places, held):
            target = pair[1] if s else dp

            def local(count=count):
                pltpu.make_async_copy(outgoing.at[count], here, o_recv.at[side]).start()

            def away(count=count, owner_id=owner_id, target=target):
                remote(
                    outgoing.at[count], here, o_send, o_recv.at[side], (owner_id, target)
                ).start()

            if (i, k, s) == (0, 0, 0):
                local()
            else:
                away()

    pending.append(lambda: wait(outgoing.at[pl.ds(0, SLOTS - 1)], o_send))
    swaps = []
    for s in range(2):
        wait(h4.at[s, :, c], o_recv.at[s])
        swaps.append(remote(h4.at[s, :, c], h4.at[s, :, c], h_send.at[s], h_recv.at[s], sibling))
        swaps[s].start()
        pending.append(swaps[s].wait_send)
    stat_copy.wait()
    for copy in swaps:
        copy.wait_recv()

    block = h4[...].reshape(BS, BS)

    @pl.when(c == 0)
    def _():
        work[...] = dot(block, block, TN)

    @pl.when(c != 0)
    def _():
        work[...] = dot(block, block, NT)

    factor = STAT_DECAY * stat[...] + (1.0 - STAT_DECAY) * work[...]
    eye = lax.broadcasted_iota(jnp.int32, (BS, BS), 0) == lax.broadcasted_iota(
        jnp.int32, (BS, BS), 1
    )
    scale = jnp.sum(jnp.where(eye, factor, 0.0)) / BS + EPSILON
    first = (jnp.where(eye, 5.0, 0.0) - factor / scale) / 4.0
    near = first.astype(BF)
    square = dot(near, near)
    rest = (5.0 * near.astype(F32) - 4.0 * square).astype(BF)
    square = square.astype(BF)
    fourth = dot(square, square).astype(BF)
    roots = []
    for k in range(2):
        rows = slice(BS // 2 * k, BS // 2 * k + BS // 2)
        moved = dot(fourth[rows], rest)
        there = rt.at[c, pl.ds(BS // 2 * k, BS // 2)]
        rt[c, pl.ds(BS // 2 * k, BS // 2), :] = ((5.0 * first[rows] - moved) / 4.0).astype(BF)
        roots.append(remote(there, there, q_send.at[k], q_recv.at[k], sibling))
        roots[k].start()
        pending.append(roots[k].wait_send)
    wide = block.astype(F32)
    grad_scale = jnp.sqrt(jnp.sum(wide * wide) / (BS * BS) + EPSILON)
    for copy in roots:
        copy.wait_recv()

    quarter = pl.ds(pl.multiple_of(128 * (2 * (1 - side) + c), 128), 128)
    carried = dot(rt[0, quarter, :], block, NT).astype(BF)
    res[1] = dot(carried, rt[1]).astype(BF)
    last = remote(res.at[1], out.at[0, 0, side], u_send.at[0], u_recv.at[0], pair)
    last.start()
    pending.append(last.wait_send)
    carried = dot(rt[0], block, NT).astype(BF)
    whole = dot(carried, rt[1])
    work[...] = whole
    quarter = pl.ds(pl.multiple_of(128 * (2 * side + c), 128), 128)
    res[0] = work[quarter, :].astype(BF)
    keep = pltpu.make_async_copy(res.at[0], out.at[0, 0, side], w_sem.at[0])
    keep.start()
    pending.append(keep.wait)
    prec_scale = jnp.sqrt(jnp.sum(whole * whole) / (BS * BS) + EPSILON)
    graft[...] = jnp.full(graft.shape, grad_scale / prec_scale, F32)
    scale_out = remote(graft, scales.at[side], u_send.at[1], u_recv.at[1], pair)
    scale_out.start()
    pending.append(scale_out.wait_send)
    keep_scale = pltpu.make_async_copy(graft, scales.at[side], w_sem.at[1])
    keep_scale.start()
    pending.append(keep_scale.wait)
    last.wait_recv()
    scale_out.wait_recv()

    for done in pending:
        done()


def shards(acts, grads_out, stats, owner, col_index):
    dma = pltpu.SemaphoreType.DMA
    smem = pl.BlockSpec(memory_space=pltpu.SMEM)
    hbm = pl.BlockSpec(memory_space=pl.ANY)
    raw, scales = pl.pallas_call(
        kernel,
        out_shape=(
            jax.ShapeDtypeStruct((1, 1, 2, 128, BS), BF),
            jax.ShapeDtypeStruct((2, 8, BS), F32),
        ),
        in_specs=[
            smem, smem, hbm, hbm, hbm
        ],
        out_specs=(hbm, hbm),
        scratch_shapes=[
            pltpu.VMEM((TOK, 128), BF),
            pltpu.VMEM((NX, 2 * NB, 16, TOK), BF),
            pltpu.VMEM((NX, 2, 2, TOK, 128), BF),
            pltpu.VMEM((NY, 2 * HALF, 128), F32),
            pltpu.VMEM((HOPS, SUB, 128), BF),
            pltpu.VMEM((HOPS, SUB, 128), BF),
            pltpu.VMEM((NE, 2, 16, 128), BF),
            pltpu.VMEM((2 * NE + 1, 16, 128), BF),
            pltpu.VMEM((SLOTS, 16, 128), BF),
            pltpu.VMEM((2, NX, 2, 32, BS), BF),
            pltpu.VMEM((2, BS, BS), BF),
            pltpu.VMEM((BS, BS), F32),
            pltpu.VMEM((BS, BS), F32),
            pltpu.VMEM((2, 128, BS), BF),
            pltpu.VMEM((8, BS), F32),
            pltpu.VMEM((2, 8, 128), jnp.int32),
            pltpu.SMEM((2, 8, 128), jnp.int32),
            dma((2, 3)), dma((2, 3)), dma(()), dma((2,)), dma((2,)), dma((2,)),
            dma(()), dma((HOPS,)), dma(()), dma(()),
            dma(()), dma((2,)), dma((2,)), dma((2,)), dma((2,)), dma((2,)), dma((2,)), dma((2,)), dma(()), dma(()),
            dma((5,)), dma((2,)), pltpu.SemaphoreType.REGULAR,
        ],
        compiler_params=pltpu.CompilerParams(
            collective_id=0, has_side_effects=True, vmem_limit_bytes=60 * 1024 * 1024
        ),
    )(owner.reshape(-1), col_index, acts, grads_out.T.reshape(NB, 2, 16, TOK), stats.reshape(BS, BS))
    scaled = raw.reshape(2, 16, 8, BS).astype(F32) * scales[:, None]
    return scaled.astype(BF).reshape(raw.shape)


def solution(mesh):
    return jax.shard_map(
        shards,
        mesh=mesh,
        in_specs=(P("own", "dp"), P("own", "dp"), P("own", "dp", None, None, None), P(), P()),
        out_specs=P("own", "dp", None, None, None),
        check_vma=False,
    )
```
